128 devices in a mesh: row: 8 (over x_lo, y), col: 16 (over z, x_hi, core).
Axes of the slice: x: 4 (x_hi: 2, x_lo: 2; x = x_hi * 2 + x_lo), y: 4, z: 4, core: 2. Of those that a mesh axis runs over, the one named last changes fastest.
Arguments:
- voltages: bfloat16 [262144, 1024], P(('row', 'col')), may hold values from -24 to 24
- filter_taps: float32 [4, 512], replicated, may hold values from -3 to 3
Outputs:
- visibilities: bfloat16 [256, 2, 1024, 1024], P(('row', 'col'))
The draws below stay inside these ranges and needn't reach their ends.
All inputs are finite; a program needn't handle non-finite values.
Results may differ from the reference program's by a relative error of at most 0.0072.
Values may be sent and summed in bfloat16 or wider, within the bound.
A program may use at most 64 MiB of HBM per device.

```python
import jax
import jax.numpy as jnp
from jax import lax

SIG = 1024
P_SIZE = 512
TAPS = 4
CH = 256
SPECTRA = 512
TIME = 262144


def strengthened(array, key, source, target, blocks, factor):
    def block_of(position):
        return (jnp.arange(array.shape[position]) // (array.shape[position] // blocks)).reshape((-1,) + (1,) * (array.ndim - 1 - position))

    one_side = jax.random.permutation(key, blocks)[block_of(target)]
    far = (block_of(target) + blocks // 2) % blocks
    return jnp.where((block_of(source) == one_side) | (block_of(source) == far), factor * array, array)


def block_scale(rng, extent, pieces, low, top_value):
    level, own = 1.0, jax.random.fold_in(rng, 6)
    for position, shards_of in pieces:
        steps = jnp.exp(jax.random.uniform(jax.random.fold_in(own, position), (shards_of,), jnp.float32, low / len(pieces), top_value / len(pieces)))
        level = level * jnp.repeat(steps, extent[position] // shards_of).reshape([-1 if axis == position else 1 for axis in range(len(extent))])
    return level


def centred(own_key, extent, scale, bound, cuts=(), kind=jnp.bfloat16):
    drawn = jax.random.normal(own_key, extent, jnp.float32) * scale
    if len(cuts) > 0:
        drawn = block_scale(own_key, extent, cuts, -0.22, 0.18) * drawn
    return jnp.clip(drawn, min=-bound, max=bound).astype(kind)


def gaussian_with(rng, shape, deviation, limit, split, heavy, kind=jnp.bfloat16):
    result = deviation * jax.random.normal(rng, shape, jnp.float32)
    if split:
        result = result * block_scale(rng, shape, split, -0.22, 0.18)
    return jnp.clip(strengthened(result, jax.random.fold_in(rng, 3), *heavy), -limit, limit).astype(kind)


def setup_inputs(seed: int = 0) -> dict:
    key_list = jax.random.split(jax.random.key(seed), 3)
    return {
        "voltages": gaussian_with(key_list[0], (TIME, SIG), 1.0, 24.0, ((0, 128),), (0, 1, 128, 5.5)),
        "filter_taps": centred(key_list[1], (TAPS, P_SIZE), 0.5, 3.0, (), jnp.float32),
    }


def fourier_table(points):
    rows = jnp.arange(points // 2, dtype=jnp.int32)[:, None]
    cols = jnp.arange(points, dtype=jnp.int32)[None, :]
    phase = (rows * cols % points).astype(jnp.float32) * (2.0 * jnp.pi / points)
    scale = 1.0 / jnp.sqrt(jnp.float32(points))
    table = jnp.concatenate([jnp.cos(phase), -jnp.sin(phase)], axis=0) * scale
    return table.astype(jnp.bfloat16)

def reference(voltages, filter_taps):
    table = fourier_table(P_SIZE)
    frames = voltages.reshape(SPECTRA, P_SIZE, SIG)
    padded = jnp.concatenate([jnp.zeros((TAPS - 1, P_SIZE, SIG), jnp.bfloat16), frames], axis=0)

    def one_frame(index):
        window = lax.dynamic_slice_in_dim(padded, index, TAPS, 0).astype(jnp.float32)
        filtered = lax.optimization_barrier(jnp.sum(filter_taps[:, :, None] * window, axis=0)).astype(jnp.bfloat16)
        return jnp.dot(table, filtered, preferred_element_type=jnp.float32).astype(jnp.bfloat16)
    spectra = lax.map(one_frame, jnp.arange(SPECTRA, dtype=jnp.int32))
    spectra = spectra.reshape(SPECTRA, 2, CH, SIG).transpose(1, 2, 0, 3)

    def one_channel(channel):
        parts = lax.dynamic_index_in_dim(spectra, channel, 1, keepdims=False)
        stacked = jnp.concatenate([parts[0], parts[1]], axis=0)
        rotated = jnp.concatenate([parts[1], -parts[0]], axis=0)
        real_part = jnp.dot(stacked.T, stacked, preferred_element_type=jnp.float32)
        imag_part = jnp.dot(rotated.T, stacked, preferred_element_type=jnp.float32)
        both = jnp.stack([real_part, imag_part], axis=0) * (1.0 / SPECTRA)
        return both.astype(jnp.bfloat16)
    return lax.map(one_channel, jnp.arange(CH, dtype=jnp.int32))
```

```python
import itertools

import jax
import jax.numpy as jnp
import numpy as np
from jax import lax
from jax.experimental import pallas as pl
from jax.experimental.pallas import tpu as pltpu
from jax.sharding import PartitionSpec as P

MESH = pl.DeviceIdType.MESH
DEVICES = 128
POINTS = 512
TAPS = 4
SPECTRA = 512
FRAMES = 8
REACH = FRAMES + TAPS - 1
HALF = 512
LANES = 128
GROUPS = HALF // LANES
TAIL = (TAPS - 1) * LANES
WIDE = 2 * HALF + TAIL


def orbit(offset):
    found = set()
    for turn in range(3):
        turned = offset[turn:] + offset[:turn]
        found.add(turned)
        found.add(tuple((-step) % 4 for step in turned))
    return tuple(sorted(found))


def send_order():
    hops = lambda group: sum(min(step, 4 - step) for step in group[0])
    groups = {orbit(offset) for offset in itertools.product(range(4), repeat=3)}
    ordered = []
    for group in sorted(sorted(groups), key=hops, reverse=True):
        for core in (0, 1):
            ordered += [offset + (core,) for offset in group]
    return [offset for offset in ordered if any(offset)]


ORDER = send_order()


def coordinates():
    row, col = lax.axis_index("row"), lax.axis_index("col")
    return ((col // 2) % 2) * 2 + row // 4, row % 4, col // 4, col % 2


def partner(offset):
    place = coordinates()
    x, y, z = ((own + step) % 4 for own, step in zip(place[:3], offset[:3]))
    core = (place[3] + offset[3]) % 2
    return (x % 2) * 4 + y, z * 4 + (x // 2) * 2 + core


def fourier_rows():
    turns = np.arange(POINTS // 2)[:, None] * np.arange(POINTS)[None, :] % POINTS
    phase = turns.astype(np.float32) * np.float32(2.0 * np.pi / POINTS)
    scale = np.float32(1.0) / np.sqrt(np.float32(POINTS))
    table = np.stack([np.cos(phase), -np.sin(phase)], axis=1) * scale
    return table.reshape(POINTS, POINTS).astype(jnp.bfloat16)


def spread(
    volt_ref, taps_ref, table_ref, out_ref,
    frames, weights, filtered, main, tails, outbox, inbox, lifted, added,
    near_sem, pair_send, pair_recv, send_sem, recv_sem, own_sem,
):
    row, col = lax.axis_index("row"), lax.axis_index("col")
    me = row * 16 + col
    core = col % 2
    barrier = pltpu.get_barrier_semaphore()
    for offset in ORDER:
        pl.semaphore_signal(barrier, inc=1, device_id=partner(offset), device_id_type=MESH)

    block = POINTS * FRAMES // 2
    mine = pl.ds(pl.multiple_of(core * HALF, HALF), HALF)
    other = pl.ds(pl.multiple_of((1 - core) * HALF, HALF), HALF)
    place = pl.ds(pl.multiple_of((TAPS - 1) * POINTS + core * block, POINTS), block)
    near = pltpu.make_async_copy(volt_ref.at[:, mine], frames.at[place], near_sem)
    near.start()
    blank = (TAPS - 1) * POINTS
    frames[0:blank, :] = jnp.zeros((blank, HALF), jnp.bfloat16)
    frames[blank + 2 * block :, :] = jnp.zeros((blank, HALF), jnp.bfloat16)
    for tap in range(TAPS):
        weights[tap] = jnp.broadcast_to(taps_ref[:, tap : tap + 1], (POINTS, LANES))
    added[...] = jnp.zeros(added.shape, jnp.float32)

    pl.semaphore_wait(barrier, len(ORDER))
    swap = pltpu.make_async_remote_copy(
        src_ref=volt_ref.at[:, other],
        dst_ref=frames.at[place],
        send_sem=pair_send,
        recv_sem=pair_recv,
        device_id=partner((0, 0, 0, 1)),
        device_id_type=MESH,
    )
    swap.start()
    near.wait()

    def one_frame(step, carry):
        frame = (step + (REACH - FRAMES // 2) * core) % REACH
        for part in range(POINTS // 64):
            rows = slice(part * 64, part * 64 + 64)
            total = jnp.zeros((64, HALF), jnp.float32)
            for tap in range(TAPS):
                start = pl.multiple_of((frame + tap) * POINTS + part * 64, 64)
                weight = jnp.concatenate([weights[tap, rows, :]] * GROUPS, axis=1)
                total = total + weight * frames[pl.ds(start, 64), :].astype(jnp.float32)
            filtered[rows, :] = total.astype(jnp.bfloat16)
        spectrum = jnp.dot(table_ref[...], filtered[...], preferred_element_type=jnp.float32)

        @pl.when(frame < FRAMES)
        def _():
            for group in range(GROUPS):
                main[group, pl.ds(frame, POINTS, stride=FRAMES), :] = spectrum[:, group * LANES : (group + 1) * LANES]

        @pl.when(frame >= FRAMES)
        def _():
            for group in range(GROUPS):
                tails[frame - FRAMES, pl.ds(group, POINTS, stride=GROUPS), :] = spectrum[
                    :, group * LANES : (group + 1) * LANES
                ]

        return carry

    lax.fori_loop(0, FRAMES // 2, one_frame, 0)
    swap.wait()
    lax.fori_loop(FRAMES // 2, REACH, one_frame, 0)

    def pack(target):
        for channel in range(2):
            rows = pl.ds(pl.multiple_of(target * 32 + channel * 16, 16), 16)
            for group in range(GROUPS):
                left = channel * HALF + group * LANES
                outbox[target, :, left : left + LANES] = main[group, rows, :].astype(jnp.bfloat16)
        rows = pl.ds(pl.multiple_of(target * 16, 16), 16)
        for late in range(TAPS - 1):
            left = 2 * HALF + late * LANES
            outbox[target, :, left : left + LANES] = tails[late, rows, :].astype(jnp.bfloat16)

    for offset in ORDER:
        to = partner(offset)
        target = to[0] * 16 + to[1]
        pack(target)
        pltpu.make_async_remote_copy(
            src_ref=outbox.at[target],
            dst_ref=inbox.at[me],
            send_sem=send_sem,
            recv_sem=recv_sem,
            device_id=to,
            device_id_type=MESH,
        ).start()
    pack(me)
    own = pltpu.make_async_copy(outbox.at[me], inbox.at[me], own_sem)
    own.start()
    own.wait()
    everything = inbox.at[pl.ds(0, DEVICES - 1)]
    pltpu.make_async_copy(everything, everything, recv_sem).wait()

    def merge(step, carry):
        half, first = step % 2, (step // 2) * 8
        for index in range(8):
            chip = first + index
            before = jnp.maximum(chip - 1, 0)
            for late in range(TAPS - 1):
                left = 2 * HALF + late * LANES
                tail = inbox[before * 2 + half, :, left : left + LANES].astype(jnp.float32)
                lifted[late, index * 16 : (index + 1) * 16, :] = jnp.where(chip > 0, tail, 0.0)
        for late in range(TAPS - 1):
            for group in range(GROUPS):
                added[group, pl.ds(late, 32, stride=8), :] = lifted[late, pl.ds(group, 32, stride=4), :]
        for index in range(8):
            for channel in range(2):
                for group in range(GROUPS):
                    left = channel * HALF + group * LANES
                    value = inbox[(first + index) * 2 + half, :, left : left + LANES].astype(jnp.float32)
                    extra = added[group, index * 32 + channel * 16 : index * 32 + channel * 16 + 16, :]
                    rows = pl.ds(pl.multiple_of((first + index) * 16, 16), 16)
                    lanes = pl.ds(pl.multiple_of(half * HALF + group * LANES, LANES), LANES)
                    out_ref[channel, rows, lanes] = (value + extra).astype(jnp.bfloat16)
        return carry

    lax.fori_loop(0, DEVICES // 8, merge, 0)
    pltpu.make_async_copy(everything, everything, send_sem).wait()


def correlate(x_ref, out_ref):
    step = pl.program_id(1)
    size = out_ref.shape[2]
    columns = pl.ds(pl.multiple_of(step * size, size), size)
    left = x_ref[0, :, columns]
    depth = left.shape[0]
    split = left.reshape(depth // 16, 2, 8, size)
    turned = jnp.concatenate([split[:, 1:], -split[:, :1]], axis=1).reshape(depth, size)
    dims = (((0,), (0,)), ((), ()))
    for part, operand in enumerate((left, turned)):
        result = lax.dot_general(operand, x_ref[0], dims, preferred_element_type=jnp.float32)
        out_ref[0, part] = (result * (1.0 / SPECTRA)).astype(jnp.bfloat16)


def shards(voltages, filter_taps):
    inputs = voltages.shape[1]
    vmem = pl.BlockSpec(memory_space=pltpu.VMEM)
    collected = pl.pallas_call(
        spread,
        name="spread",
        out_shape=jax.ShapeDtypeStruct((2, 2 * SPECTRA, inputs), jnp.bfloat16),
        in_specs=[pl.BlockSpec(memory_space=pl.ANY), vmem, vmem],
        out_specs=vmem,
        scratch_shapes=[
            pltpu.VMEM(((FRAMES + 2 * TAPS - 2) * POINTS, HALF), jnp.bfloat16),
            pltpu.VMEM((TAPS, POINTS, LANES), jnp.float32),
            pltpu.VMEM((POINTS, HALF), jnp.bfloat16),
            pltpu.VMEM((GROUPS, POINTS * FRAMES, LANES), jnp.float32),
            pltpu.VMEM((TAPS - 1, POINTS * GROUPS, LANES), jnp.float32),
            pltpu.VMEM((DEVICES, 16, WIDE), jnp.bfloat16),
            pltpu.VMEM((DEVICES, 16, WIDE), jnp.bfloat16),
            pltpu.VMEM((TAPS - 1, LANES, LANES), jnp.float32),
            pltpu.VMEM((GROUPS, 256, LANES), jnp.float32),
        ]
        + [pltpu.SemaphoreType.DMA(())] * 6,
        compiler_params=pltpu.CompilerParams(
            collective_id=0, has_side_effects=True, vmem_limit_bytes=58 << 20
        ),
    )(voltages, filter_taps.T, jnp.asarray(fourier_rows()))
    size = 256
    return pl.pallas_call(
        correlate,
        name="correlate",
        grid=(2, inputs // size),
        out_shape=jax.ShapeDtypeStruct((2, 2, inputs, inputs), jnp.bfloat16),
        in_specs=[pl.BlockSpec((1, 2 * SPECTRA, inputs), lambda channel, step: (channel, 0, 0))],
        out_specs=pl.BlockSpec((1, 2, size, inputs), lambda channel, step: (channel, 0, step, 0)),
        compiler_params=pltpu.CompilerParams(vmem_limit_bytes=58 << 20),
    )(collected)


def solution(mesh):
    placed = (P(("row", "col"), None), P())
    return jax.shard_map(
        shards,
        mesh=mesh,
        in_specs=placed,
        out_specs=P(("row", "col"), None, None, None),
        check_vma=False,
    )
```

```python
import itertools

import jax
import jax.numpy as jnp
import numpy as np
from jax import lax
from jax.experimental import pallas as pl
from jax.experimental.pallas import tpu as pltpu
from jax.sharding import PartitionSpec as P

MESH = pl.DeviceIdType.MESH
DEVICES = 128
POINTS = 512
TAPS = 4
SPECTRA = 512
OWN = 4
LATE = TAPS - 1
SIGNALS = 1024
HALF = SIGNALS // 2
LANES = 128
GROUPS = SIGNALS // LANES
BLOCK = 256


def orbit(offset):
    found = set()
    for turn in range(3):
        turned = offset[turn:] + offset[:turn]
        found.add(turned)
        found.add(tuple((-step) % 4 for step in turned))
    return tuple(sorted(found))


def send_order():
    hops = lambda group: sum(min(step, 4 - step) for step in group[0])
    groups = {orbit(offset) for offset in itertools.product(range(4), repeat=3)}
    ordered = []
    for group in sorted(sorted(groups), key=hops, reverse=True):
        for core in (0, 1):
            ordered += [offset + (core,) for offset in group]
    return [offset for offset in ordered if any(offset)]


ORDER = send_order()


def coordinates():
    row, col = lax.axis_index("row"), lax.axis_index("col")
    return ((col // 2) % 2) * 2 + row // 4, row % 4, col // 4, col % 2


def partner(offset):
    place = coordinates()
    x, y, z = ((own + step) % 4 for own, step in zip(place[:3], offset[:3]))
    core = (place[3] + offset[3]) % 2
    return (x % 2) * 4 + y, z * 4 + (x // 2) * 2 + core


def fourier_rows():
    turns = np.arange(POINTS // 2)[:, None] * np.arange(POINTS)[None, :] % POINTS
    phase = turns.astype(np.float32) * np.float32(2.0 * np.pi / POINTS)
    scale = np.float32(1.0) / np.sqrt(np.float32(POINTS))
    table = np.stack([np.cos(phase), -np.sin(phase)], axis=1) * scale
    table = table.reshape(DEVICES, 2, 2, POINTS).transpose(1, 0, 2, 3)
    return table.reshape(2, POINTS // 2, POINTS).astype(jnp.bfloat16)


def correlate(x_ref, y_ref, result, out_ref, sem):
    dims = (((0,), (0,)), ((), ()))
    copies = []
    for step in range(SIGNALS // BLOCK):
        first, after = step * BLOCK, (step + 1) * BLOCK
        for part, left in enumerate((x_ref, y_ref)):
            product = lax.dot_general(
                left[:, first:after], x_ref[:, first:], dims, preferred_element_type=jnp.float32
            )
            product = product * (1.0 / SPECTRA)
            result[part, first:after, first:] = product.astype(jnp.bfloat16)
            if after < SIGNALS:
                mirror = product[:, BLOCK:].T if part == 0 else -product[:, BLOCK:].T
                result[part, after:, first:after] = mirror.astype(jnp.bfloat16)
        rows = pl.ds(first, BLOCK)
        copy = pltpu.make_async_copy(result.at[:, rows], out_ref.at[:, rows], sem.at[step])
        copy.start()
        copies.append(copy)
    return copies


def spread(
    volt_ref, taps_ref, table_ref, vis_ref, x_out, y_out,
    frames, weights, filtered, main, tails, outbox, outbox_late, inbox, inbox_late, lifted, added, x_ref, y_ref, result,
    near_sem, pair_sem, send_sem, recv_sem, out_sem,
):
    row, col = lax.axis_index("row"), lax.axis_index("col")
    me = row * 16 + col
    core = col % 2
    barrier = pltpu.get_barrier_semaphore()
    for offset in ORDER:
        pl.semaphore_signal(barrier, inc=1, device_id=partner(offset), device_id_type=MESH)

    near = pltpu.make_async_copy(volt_ref, frames.at[pl.ds(LATE * POINTS, OWN * POINTS)], near_sem)
    near.start()
    for tap in range(TAPS):
        weights[tap] = jnp.broadcast_to(taps_ref[:, tap : tap + 1], (POINTS, LANES))
    added[...] = jnp.zeros(added.shape, jnp.float32)
    halo = pltpu.make_async_remote_copy(
        src_ref=volt_ref.at[pl.ds((OWN - LATE) * POINTS, LATE * POINTS)],
        dst_ref=frames.at[pl.ds(0, LATE * POINTS)],
        send_sem=pair_sem.at[0],
        recv_sem=pair_sem.at[1],
        device_id=partner((0, 0, 0, 1)),
        device_id_type=MESH,
    )

    def filter_frames(outputs, slots):
        def rows16(step, carry):
            rows = pl.ds(pl.multiple_of(step * 16, 16), 16)
            taps = [jnp.concatenate([weights[tap, rows, :]] * 2, axis=1) for tap in range(TAPS)]
            for left in range(0, SIGNALS, 256):
                lanes = slice(left, left + 256)
                values = {}
                for slot in slots:
                    at = pl.ds(pl.multiple_of(slot * POINTS + step * 16, 16), 16)
                    values[slot] = frames[at, lanes].astype(jnp.float32)
                for frame in outputs:
                    total = None
                    for tap in range(TAPS):
                        if frame + tap in values:
                            term = taps[tap] * values[frame + tap]
                            total = term if total is None else total + term
                    filtered[frame, rows, lanes] = total.astype(jnp.bfloat16)
            return carry

        lax.fori_loop(0, POINTS // 16, rows16, 0)

    def transform(channel, index, frame):
        half = index % 2
        lanes = pl.ds(pl.multiple_of(half * HALF, HALF), HALF)
        return half, jnp.dot(table_ref[channel], filtered[frame, :, lanes], preferred_element_type=jnp.float32)

    def transform_main(channel):
        def one(index, carry):
            frame = index // 2
            half, spectrum = transform(channel, index, frame)
            for group in range(GROUPS // 2):
                rows = pl.ds(frame, 2 * DEVICES, stride=OWN)
                main[half * (GROUPS // 2) + group, rows, :] = spectrum[:, group * LANES : (group + 1) * LANES]
            return carry

        lax.fori_loop(0, 2 * OWN, one, 0)

    def transform_late(channel):
        def one(index, carry):
            late = index // 2
            half, spectrum = transform(channel, index, late + OWN)
            for group in range(GROUPS // 2):
                rows = pl.ds(half * (GROUPS // 2) + group, 2 * DEVICES, stride=GROUPS)
                tails[late, rows, :] = spectrum[:, group * LANES : (group + 1) * LANES]
            return carry

        lax.fori_loop(0, 2 * LATE, one, 0)

    def pack_main(channel):
        def one(target, carry):
            rows = pl.ds(pl.multiple_of(target * 8, 8), 8)
            for group in range(GROUPS // 2):
                both = jnp.concatenate([main[group, rows, :], main[group + GROUPS // 2, rows, :]], axis=0)
                outbox[channel, target, :, group * LANES : (group + 1) * LANES] = both.astype(jnp.bfloat16)
            return carry

        lax.fori_loop(0, DEVICES, one, 0, unroll=4)

    def pack_late(channel):
        def one(target, carry):
            rows = pl.ds(pl.multiple_of(target * 16, 16), 16)
            for late in range(LATE):
                outbox_late[channel, target, :, late * LANES : (late + 1) * LANES] = tails[late, rows, :].astype(
                    jnp.bfloat16
                )
            return carry

        lax.fori_loop(0, DEVICES, one, 0, unroll=4)

    def send(channel, box, into, place, sem):
        for offset in ORDER:
            to = partner(offset)
            pltpu.make_async_remote_copy(
                src_ref=box.at[channel, to[0] * 16 + to[1]],
                dst_ref=into.at[channel, place],
                send_sem=send_sem.at[sem],
                recv_sem=recv_sem.at[sem],
                device_id=to,
                device_id_type=MESH,
            ).start()

    def send_main(channel):
        pack_main(channel)
        send(channel, outbox, inbox, me, channel)
        inbox[channel, me] = outbox[channel, me]

    def send_late(channel):
        pack_late(channel)
        send(channel, outbox_late, inbox_late, me // 2, 2 + channel)
        inbox_late[channel, me // 2] = outbox_late[channel, me]

    def arrived(channel):
        most = inbox.at[channel, pl.ds(0, DEVICES - 1)]
        pltpu.make_async_copy(most, most, recv_sem.at[channel]).wait()

        @pl.when(core == 0)
        def _():
            late = inbox_late.at[channel]
            pltpu.make_async_copy(late, late, recv_sem.at[2 + channel]).wait()

        @pl.when(core == 1)
        def _():
            late = inbox_late.at[channel, pl.ds(0, DEVICES // 2 - 1)]
            pltpu.make_async_copy(late, late, recv_sem.at[2 + channel]).wait()

    def merge(channel):
        row_of = lax.broadcasted_iota(jnp.int32, (16, LANES), 0)
        sign = jnp.where(row_of % 8 < OWN, 1.0, -1.0).astype(jnp.float32)

        def eight(step, carry):
            first = step * 8
            for index in range(8):
                chip = first + index
                before = jnp.maximum(chip - 1, 0)
                for late in range(LATE):
                    tail = inbox_late[channel, before, :, late * LANES : (late + 1) * LANES].astype(jnp.float32)
                    lifted[late, index * 16 : (index + 1) * 16, :] = jnp.where(chip > 0, tail, 0.0)
            for late in range(LATE):
                for group in range(GROUPS):
                    added[group, pl.ds(late, 16, stride=OWN), :] = lifted[late, pl.ds(group, 16, stride=GROUPS), :]
            for index in range(8):
                chip = first + index
                rows = pl.ds(pl.multiple_of(chip * 16, 16), 16)
                for group in range(GROUPS // 2):
                    lanes = slice(group * LANES, (group + 1) * LANES)
                    lower = inbox[channel, 2 * chip, :, lanes].astype(jnp.float32)
                    upper = inbox[channel, 2 * chip + 1, :, lanes].astype(jnp.float32)
                    for half in range(2):
                        whole = half * (GROUPS // 2) + group
                        extra = added[whole, index * 8 : index * 8 + 8, :]
                        part = slice(half * 8, half * 8 + 8)
                        early = lower[part] + extra
                        value = jnp.concatenate([early, upper[part]], axis=0)
                        turned = jnp.concatenate(
                            [pltpu.roll(early, OWN, 0), pltpu.roll(upper[part], OWN, 0)], axis=0
                        )
                        out = slice(whole * LANES, (whole + 1) * LANES)
                        x_ref[rows, out] = value.astype(jnp.bfloat16)
                        y_ref[rows, out] = (turned * sign).astype(jnp.bfloat16)
            return carry

        lax.fori_loop(0, DEVICES // 16, eight, 0)

    @pl.when(core == 0)
    def _():
        pl.semaphore_wait(barrier, len(ORDER))
        halo.start()
        frames[0 : LATE * POINTS, :] = jnp.zeros((LATE * POINTS, SIGNALS), jnp.bfloat16)
        near.wait()

    @pl.when(core == 1)
    def _():
        near.wait()
        filter_frames(range(OWN, OWN + LATE), range(OWN, OWN + LATE))
        transform_late(0)
        pl.semaphore_wait(barrier, len(ORDER))
        send_late(0)
        halo.wait_recv()

    filter_frames(range(OWN), range(OWN + LATE))
    transform_main(0)
    send_main(0)

    @pl.when(core == 1)
    def _():
        transform_late(1)
        send_late(1)

    transform_main(1)
    send_main(1)

    arrived(0)
    merge(0)
    copies = correlate(x_ref, y_ref, result, vis_ref, out_sem)
    arrived(1)
    merge(1)
    copies.append(pltpu.make_async_copy(x_ref, x_out, out_sem.at[4]))
    copies.append(pltpu.make_async_copy(y_ref, y_out, out_sem.at[5]))
    copies[-2].start()
    copies[-1].start()
    for channel in range(2):
        most = outbox.at[channel, pl.ds(0, DEVICES - 1)]
        pltpu.make_async_copy(most, most, send_sem.at[channel]).wait()

    @pl.when(core == 0)
    def _():
        halo.wait_send()

    @pl.when(core == 1)
    def _():
        for channel in range(2):
            most = outbox_late.at[channel, pl.ds(0, DEVICES - 1)]
            pltpu.make_async_copy(most, most, send_sem.at[2 + channel]).wait()

    for copy in copies:
        copy.wait()


def finish(vis_ref, x_in, y_in, out_ref, x_ref, y_ref, result, in_sem, out_sem):
    loads = [
        pltpu.make_async_copy(x_in, x_ref, in_sem.at[0]),
        pltpu.make_async_copy(y_in, y_ref, in_sem.at[1]),
    ]
    for load in loads:
        load.start()
    for load in loads:
        load.wait()
    done = pltpu.make_async_copy(vis_ref, out_ref.at[0], in_sem.at[2])
    done.start()
    for copy in correlate(x_ref, y_ref, result, out_ref.at[1], out_sem):
        copy.wait()
    done.wait()


def shards(voltages, filter_taps):
    inputs = voltages.shape[1]
    vmem = pl.BlockSpec(memory_space=pltpu.VMEM)
    anywhere = pl.BlockSpec(memory_space=pl.ANY)
    bf16, f32 = jnp.bfloat16, jnp.float32
    square = jax.ShapeDtypeStruct((2 * SPECTRA, inputs), bf16)
    one, x, y = pl.pallas_call(
        spread,
        name="spread",
        out_shape=[jax.ShapeDtypeStruct((2, inputs, inputs), bf16), square, square],
        in_specs=[anywhere, vmem, vmem],
        out_specs=[anywhere] * 3,
        scratch_shapes=[
            pltpu.VMEM(((OWN + LATE) * POINTS, SIGNALS), bf16),
            pltpu.VMEM((TAPS, POINTS, LANES), f32),
            pltpu.VMEM((OWN + LATE, POINTS, SIGNALS), bf16),
            pltpu.VMEM((GROUPS, DEVICES * 2 * OWN, LANES), f32),
            pltpu.VMEM((LATE, DEVICES * 2 * GROUPS, LANES), f32),
            pltpu.VMEM((2, DEVICES, 16, HALF), bf16),
            pltpu.VMEM((2, DEVICES, 16, LATE * LANES), bf16),
            pltpu.VMEM((2, DEVICES, 16, HALF), bf16),
            pltpu.VMEM((2, DEVICES // 2, 16, LATE * LANES), bf16),
            pltpu.VMEM((LATE, 128, LANES), f32),
            pltpu.VMEM((GROUPS, 64, LANES), f32),
            pltpu.VMEM((2 * SPECTRA, SIGNALS), bf16),
            pltpu.VMEM((2 * SPECTRA, SIGNALS), bf16),
            pltpu.VMEM((2, SIGNALS, SIGNALS), bf16),
            pltpu.SemaphoreType.DMA(()),
            pltpu.SemaphoreType.DMA((2,)),
            pltpu.SemaphoreType.DMA((4,)),
            pltpu.SemaphoreType.DMA((4,)),
            pltpu.SemaphoreType.DMA((6,)),
        ],
        compiler_params=pltpu.CompilerParams(
            collective_id=0, has_side_effects=True, vmem_limit_bytes=58 << 20
        ),
    )(voltages, filter_taps.T, jnp.asarray(fourier_rows()))
    return pl.pallas_call(
        finish,
        name="finish",
        out_shape=jax.ShapeDtypeStruct((2, 2, inputs, inputs), bf16),
        in_specs=[anywhere] * 3,
        out_specs=anywhere,
        scratch_shapes=[
            pltpu.VMEM((2 * SPECTRA, SIGNALS), bf16),
            pltpu.VMEM((2 * SPECTRA, SIGNALS), bf16),
            pltpu.VMEM((2, SIGNALS, SIGNALS), bf16),
            pltpu.SemaphoreType.DMA((3,)),
            pltpu.SemaphoreType.DMA((SIGNALS // BLOCK,)),
        ],
        compiler_params=pltpu.CompilerParams(vmem_limit_bytes=60 << 20),
    )(one, x, y)


def solution(mesh):
    placed = (P(("row", "col"), None), P())
    return jax.shard_map(
        shards,
        mesh=mesh,
        in_specs=placed,
        out_specs=P(("row", "col"), None, None, None),
        check_vma=False,
    )
```

```python
import itertools

import jax
import jax.numpy as jnp
import numpy as np
from jax import lax
from jax.experimental import pallas as pl
from jax.experimental.pallas import tpu as pltpu
from jax.sharding import PartitionSpec as P

MESH = pl.DeviceIdType.MESH
DEVICES = 128
POINTS = 512
TAPS = 4
SPECTRA = 512
OWN = 4
LATE = TAPS - 1
SIGNALS = 1024
HALF = SIGNALS // 2
LANES = 128
GROUPS = SIGNALS // LANES
BLOCK = 256


def orbit(offset):
    found = set()
    for turn in range(3):
        turned = offset[turn:] + offset[:turn]
        found.add(turned)
        found.add(tuple((-step) % 4 for step in turned))
    return tuple(sorted(found))


def send_order():
    hops = lambda group: sum(min(step, 4 - step) for step in group[0])
    groups = {orbit(offset) for offset in itertools.product(range(4), repeat=3)}
    ordered = []
    for group in sorted(sorted(groups), key=hops, reverse=True):
        for core in (0, 1):
            ordered += [offset + (core,) for offset in group]
    return [offset for offset in ordered if any(offset)]


ORDER = send_order()


def coordinates():
    row, col = lax.axis_index("row"), lax.axis_index("col")
    return ((col // 2) % 2) * 2 + row // 4, row % 4, col // 4, col % 2


def partner(offset):
    place = coordinates()
    x, y, z = ((own + step) % 4 for own, step in zip(place[:3], offset[:3]))
    core = (place[3] + offset[3]) % 2
    return (x % 2) * 4 + y, z * 4 + (x // 2) * 2 + core


def fourier_rows():
    turns = np.arange(POINTS // 2)[:, None] * np.arange(POINTS)[None, :] % POINTS
    phase = turns.astype(np.float32) * np.float32(2.0 * np.pi / POINTS)
    scale = np.float32(1.0) / np.sqrt(np.float32(POINTS))
    table = np.stack([np.cos(phase), -np.sin(phase)], axis=1) * scale
    table = table.reshape(DEVICES, 2, 2, POINTS).transpose(1, 0, 2, 3)
    return table.reshape(2, POINTS // 2, POINTS).astype(jnp.bfloat16)


def correlate(x_ref, y_ref, result, out_ref, sem):
    dims = (((0,), (0,)), ((), ()))
    copies = []
    for step in range(SIGNALS // BLOCK):
        first, after = step * BLOCK, (step + 1) * BLOCK
        for part, left in enumerate((x_ref, y_ref)):
            product = lax.dot_general(
                left[:, first:after], x_ref[:, first:], dims, preferred_element_type=jnp.float32
            )
            product = product * (1.0 / SPECTRA)
            result[part, first:after, first:] = product.astype(jnp.bfloat16)
            if after < SIGNALS:
                mirror = product[:, BLOCK:].T if part == 0 else -product[:, BLOCK:].T
                result[part, after:, first:after] = mirror.astype(jnp.bfloat16)
        rows = pl.ds(first, BLOCK)
        copy = pltpu.make_async_copy(result.at[:, rows], out_ref.at[:, rows], sem.at[step])
        copy.start()
        copies.append(copy)
    return copies


def spread(
    volt_ref, taps_ref, table_ref, vis_ref, x_out, y_out,
    frames, weights, filtered, main, tails, outbox, outbox_late, inbox, inbox_late, lifted, added, x_ref, y_ref, result,
    near_sem, pair_sem, send_sem, recv_sem, out_sem,
):
    row, col = lax.axis_index("row"), lax.axis_index("col")
    me = row * 16 + col
    core = col % 2
    barrier = pltpu.get_barrier_semaphore()
    for offset in ORDER:
        pl.semaphore_signal(barrier, inc=1, device_id=partner(offset), device_id_type=MESH)

    near = pltpu.make_async_copy(volt_ref, frames.at[pl.ds(LATE * POINTS, OWN * POINTS)], near_sem)
    near.start()
    for tap in range(TAPS):
        weights[tap] = jnp.broadcast_to(taps_ref[:, tap : tap + 1], (POINTS, LANES))
    added[...] = jnp.zeros(added.shape, jnp.float32)
    halo = pltpu.make_async_remote_copy(
        src_ref=volt_ref.at[pl.ds((OWN - LATE) * POINTS, LATE * POINTS)],
        dst_ref=frames.at[pl.ds(0, LATE * POINTS)],
        send_sem=pair_sem.at[0],
        recv_sem=pair_sem.at[1],
        device_id=partner((0, 0, 0, 1)),
        device_id_type=MESH,
    )

    def filter_frames(outputs, slots):
        def rows16(step, carry):
            rows = pl.ds(pl.multiple_of(step * 16, 16), 16)
            taps = [jnp.concatenate([weights[tap, rows, :]] * 2, axis=1) for tap in range(TAPS)]
            for left in range(0, SIGNALS, 256):
                lanes = slice(left, left + 256)
                values = {}
                for slot in slots:
                    at = pl.ds(pl.multiple_of(slot * POINTS + step * 16, 16), 16)
                    values[slot] = frames[at, lanes].astype(jnp.float32)
                for frame in outputs:
                    total = None
                    for tap in range(TAPS):
                        if frame + tap in values:
                            term = taps[tap] * values[frame + tap]
                            total = term if total is None else total + term
                    filtered[frame, rows, lanes] = total.astype(jnp.bfloat16)
            return carry

        lax.fori_loop(0, POINTS // 16, rows16, 0)

    def transform(channel, index, frame):
        half = index % 2
        lanes = pl.ds(pl.multiple_of(half * HALF, HALF), HALF)
        return half, jnp.dot(table_ref[channel], filtered[frame, :, lanes], preferred_element_type=jnp.float32)

    def transform_main(channel):
        def one(index, carry):
            frame = index // 2
            half, spectrum = transform(channel, index, frame)
            for group in range(GROUPS // 2):
                rows = pl.ds(frame, 2 * DEVICES, stride=OWN)
                main[half * (GROUPS // 2) + group, rows, :] = spectrum[:, group * LANES : (group + 1) * LANES]
            return carry

        lax.fori_loop(0, 2 * OWN, one, 0)

    def transform_late(channel):
        def one(index, carry):
            late = index // 2
            half, spectrum = transform(channel, index, late + OWN)
            for group in range(GROUPS // 2):
                rows = pl.ds(half * (GROUPS // 2) + group, 2 * DEVICES, stride=GROUPS)
                tails[late, rows, :] = spectrum[:, group * LANES : (group + 1) * LANES]
            return carry

        lax.fori_loop(0, 2 * LATE, one, 0)

    def pack_main(channel):
        def one(target, carry):
            rows = pl.ds(pl.multiple_of(target * 8, 8), 8)
            for group in range(GROUPS // 2):
                both = jnp.concatenate([main[group, rows, :], main[group + GROUPS // 2, rows, :]], axis=0)
                outbox[channel, target, :, group * LANES : (group + 1) * LANES] = both.astype(jnp.bfloat16)
            return carry

        lax.fori_loop(0, DEVICES, one, 0, unroll=4)

    def pack_late(channel):
        def one(target, carry):
            rows = pl.ds(pl.multiple_of(target * 16, 16), 16)
            for late in range(LATE):
                outbox_late[channel, target, :, late * LANES : (late + 1) * LANES] = tails[late, rows, :].astype(
                    jnp.bfloat16
                )
            return carry

        lax.fori_loop(0, DEVICES, one, 0, unroll=4)

    def send(channel, box, into, place, sem):
        for offset in ORDER:
            to = partner(offset)
            pltpu.make_async_remote_copy(
                src_ref=box.at[channel, to[0] * 16 + to[1]],
                dst_ref=into.at[channel, place],
                send_sem=send_sem.at[sem],
                recv_sem=recv_sem.at[sem],
                device_id=to,
                device_id_type=MESH,
            ).start()

    def send_main(channel):
        pack_main(channel)
        send(channel, outbox, inbox, me, channel)
        inbox[channel, me] = outbox[channel, me]

    def send_late(channel):
        pack_late(channel)
        send(channel, outbox_late, inbox_late, me // 2, 2 + channel)
        inbox_late[channel, me // 2] = outbox_late[channel, me]

    def arrived(channel):
        most = inbox.at[channel, pl.ds(0, DEVICES - 1)]
        pltpu.make_async_copy(most, most, recv_sem.at[channel]).wait()

        @pl.when(core == 0)
        def _():
            late = inbox_late.at[channel]
            pltpu.make_async_copy(late, late, recv_sem.at[2 + channel]).wait()

        @pl.when(core == 1)
        def _():
            late = inbox_late.at[channel, pl.ds(0, DEVICES // 2 - 1)]
            pltpu.make_async_copy(late, late, recv_sem.at[2 + channel]).wait()

    def merge(channel):
        row_of = lax.broadcasted_iota(jnp.int32, (16, LANES), 0)
        sign = jnp.where(row_of % 8 < OWN, 1.0, -1.0).astype(jnp.float32)

        def eight(step, carry):
            first = step * 8
            for index in range(8):
                chip = first + index
                before = jnp.maximum(chip - 1, 0)
                for late in range(LATE):
                    tail = inbox_late[channel, before, :, late * LANES : (late + 1) * LANES].astype(jnp.float32)
                    lifted[late, index * 16 : (index + 1) * 16, :] = jnp.where(chip > 0, tail, 0.0)
            for late in range(LATE):
                for group in range(GROUPS):
                    added[group, pl.ds(late, 16, stride=OWN), :] = lifted[late, pl.ds(group, 16, stride=GROUPS), :]
            for index in range(8):
                chip = first + index
                rows = pl.ds(pl.multiple_of(chip * 16, 16), 16)
                for group in range(GROUPS // 2):
                    lanes = slice(group * LANES, (group + 1) * LANES)
                    lower = inbox[channel, 2 * chip, :, lanes].astype(jnp.float32)
                    upper = inbox[channel, 2 * chip + 1, :, lanes].astype(jnp.float32)
                    for half in range(2):
                        whole = half * (GROUPS // 2) + group
                        extra = added[whole, index * 8 : index * 8 + 8, :]
                        part = slice(half * 8, half * 8 + 8)
                        early = lower[part] + extra
                        value = jnp.concatenate([early, upper[part]], axis=0)
                        turned = jnp.concatenate(
                            [pltpu.roll(early, OWN, 0), pltpu.roll(upper[part], OWN, 0)], axis=0
                        )
                        out = slice(whole * LANES, (whole + 1) * LANES)
                        x_ref[rows, out] = value.astype(jnp.bfloat16)
                        y_ref[rows, out] = (turned * sign).astype(jnp.bfloat16)
            return carry

        lax.fori_loop(0, DEVICES // 16, eight, 0)

    @pl.when(core == 0)
    def _():
        pl.semaphore_wait(barrier, len(ORDER))
        halo.start()
        frames[0 : LATE * POINTS, :] = jnp.zeros((LATE * POINTS, SIGNALS), jnp.bfloat16)
        near.wait()

    @pl.when(core == 1)
    def _():
        near.wait()
        filter_frames(range(OWN, OWN + LATE), range(OWN, OWN + LATE))
        transform_late(0)
        pl.semaphore_wait(barrier, len(ORDER))
        send_late(0)
        halo.wait_recv()

    filter_frames(range(OWN), range(OWN + LATE))
    transform_main(0)
    send_main(0)

    @pl.when(core == 1)
    def _():
        transform_late(1)
        send_late(1)

    transform_main(1)
    send_main(1)

    arrived(0)
    merge(0)
    copies = correlate(x_ref, y_ref, result, vis_ref, out_sem)
    arrived(1)
    merge(1)
    copies.append(pltpu.make_async_copy(x_ref, x_out, out_sem.at[4]))
    copies.append(pltpu.make_async_copy(y_ref, y_out, out_sem.at[5]))
    copies[-2].start()
    copies[-1].start()
    for channel in range(2):
        most = outbox.at[channel, pl.ds(0, DEVICES - 1)]
        pltpu.make_async_copy(most, most, send_sem.at[channel]).wait()

    @pl.when(core == 0)
    def _():
        halo.wait_send()

    @pl.when(core == 1)
    def _():
        for channel in range(2):
            most = outbox_late.at[channel, pl.ds(0, DEVICES - 1)]
            pltpu.make_async_copy(most, most, send_sem.at[2 + channel]).wait()

    for copy in copies:
        copy.wait()


def finish(vis_ref, x_in, y_in, out_ref, x_ref, y_ref, through, result, in_sem, out_sem):
    loads = [
        pltpu.make_async_copy(x_in, x_ref, in_sem.at[0]),
        pltpu.make_async_copy(y_in, y_ref, in_sem.at[1]),
    ]
    for load in loads:
        load.start()
    half = pltpu.make_async_copy(vis_ref, through, in_sem.at[2])
    half.start()
    for load in loads:
        load.wait()
    copies = correlate(x_ref, y_ref, result, out_ref.at[1], out_sem)
    half.wait()
    done = pltpu.make_async_copy(through, out_ref.at[0], in_sem.at[3])
    done.start()
    for copy in copies:
        copy.wait()
    done.wait()


def shards(voltages, filter_taps):
    inputs = voltages.shape[1]
    vmem = pl.BlockSpec(memory_space=pltpu.VMEM)
    anywhere = pl.BlockSpec(memory_space=pl.ANY)
    bf16, f32 = jnp.bfloat16, jnp.float32
    square = jax.ShapeDtypeStruct((2 * SPECTRA, inputs), bf16)
    one, x, y = pl.pallas_call(
        spread,
        name="spread",
        out_shape=[jax.ShapeDtypeStruct((2, inputs, inputs), bf16), square, square],
        in_specs=[anywhere, vmem, vmem],
        out_specs=[anywhere] * 3,
        scratch_shapes=[
            pltpu.VMEM(((OWN + LATE) * POINTS, SIGNALS), bf16),
            pltpu.VMEM((TAPS, POINTS, LANES), f32),
            pltpu.VMEM((OWN + LATE, POINTS, SIGNALS), bf16),
            pltpu.VMEM((GROUPS, DEVICES * 2 * OWN, LANES), f32),
            pltpu.VMEM((LATE, DEVICES * 2 * GROUPS, LANES), f32),
            pltpu.VMEM((2, DEVICES, 16, HALF), bf16),
            pltpu.VMEM((2, DEVICES, 16, LATE * LANES), bf16),
            pltpu.VMEM((2, DEVICES, 16, HALF), bf16),
            pltpu.VMEM((2, DEVICES // 2, 16, LATE * LANES), bf16),
            pltpu.VMEM((LATE, 128, LANES), f32),
            pltpu.VMEM((GROUPS, 64, LANES), f32),
            pltpu.VMEM((2 * SPECTRA, SIGNALS), bf16),
            pltpu.VMEM((2 * SPECTRA, SIGNALS), bf16),
            pltpu.VMEM((2, SIGNALS, SIGNALS), bf16),
            pltpu.SemaphoreType.DMA(()),
            pltpu.SemaphoreType.DMA((2,)),
            pltpu.SemaphoreType.DMA((4,)),
            pltpu.SemaphoreType.DMA((4,)),
            pltpu.SemaphoreType.DMA((6,)),
        ],
        compiler_params=pltpu.CompilerParams(
            collective_id=0, has_side_effects=True, vmem_limit_bytes=58 << 20
        ),
    )(voltages, filter_taps.T, jnp.asarray(fourier_rows()))
    return pl.pallas_call(
        finish,
        name="finish",
        out_shape=jax.ShapeDtypeStruct((2, 2, inputs, inputs), bf16),
        in_specs=[anywhere] * 3,
        out_specs=anywhere,
        scratch_shapes=[
            pltpu.VMEM((2 * SPECTRA, SIGNALS), bf16),
            pltpu.VMEM((2 * SPECTRA, SIGNALS), bf16),
            pltpu.VMEM((2, SIGNALS, SIGNALS), bf16),
            pltpu.VMEM((2, SIGNALS, SIGNALS), bf16),
            pltpu.SemaphoreType.DMA((4,)),
            pltpu.SemaphoreType.DMA((SIGNALS // BLOCK,)),
        ],
        compiler_params=pltpu.CompilerParams(vmem_limit_bytes=60 << 20),
    )(one, x, y)


def solution(mesh):
    placed = (P(("row", "col"), None), P())
    return jax.shard_map(
        shards,
        mesh=mesh,
        in_specs=placed,
        out_specs=P(("row", "col"), None, None, None),
        check_vma=False,
    )
```

```python
import itertools

import jax
import jax.numpy as jnp
import numpy as np
from jax import lax
from jax.experimental import pallas as pl
from jax.experimental.pallas import tpu as pltpu
from jax.sharding import PartitionSpec as P

MESH = pl.DeviceIdType.MESH
DEVICES = 128
POINTS = 512
TAPS = 4
SPECTRA = 512
OWN = 4
LATE = TAPS - 1
SIGNALS = 1024
HALF = SIGNALS // 2
LANES = 128
GROUPS = SIGNALS // LANES
BLOCK = 256


def orbit(offset):
    found = set()
    for turn in range(3):
        turned = offset[turn:] + offset[:turn]
        found.add(turned)
        found.add(tuple((-step) % 4 for step in turned))
    return tuple(sorted(found))


def send_order():
    hops = lambda group: sum(min(step, 4 - step) for step in group[0])
    groups = {orbit(offset) for offset in itertools.product(range(4), repeat=3)}
    ordered = []
    for group in sorted(sorted(groups), key=hops, reverse=True):
        for core in (0, 1):
            ordered += [offset + (core,) for offset in group]
    return [offset for offset in ordered if any(offset)]


ORDER = send_order()


def coordinates():
    row, col = lax.axis_index("row"), lax.axis_index("col")
    return ((col // 2) % 2) * 2 + row // 4, row % 4, col // 4, col % 2


def partner(offset):
    place = coordinates()
    x, y, z = ((own + step) % 4 for own, step in zip(place[:3], offset[:3]))
    core = (place[3] + offset[3]) % 2
    return (x % 2) * 4 + y, z * 4 + (x // 2) * 2 + core


def fourier_rows():
    turns = np.arange(POINTS // 2)[:, None] * np.arange(POINTS)[None, :] % POINTS
    phase = turns.astype(np.float32) * np.float32(2.0 * np.pi / POINTS)
    scale = np.float32(1.0) / np.sqrt(np.float32(POINTS))
    table = np.stack([np.cos(phase), -np.sin(phase)], axis=1) * scale
    table = table.reshape(DEVICES, 2, 2, POINTS).transpose(1, 0, 2, 3)
    return table.reshape(2, POINTS // 2, POINTS).astype(jnp.bfloat16)


def correlate(x_ref, y_ref, result, out_ref=None, sem=None):
    dims = (((0,), (0,)), ((), ()))
    copies = []
    for step in range(SIGNALS // BLOCK):
        first, after = step * BLOCK, (step + 1) * BLOCK
        for part, left in enumerate((x_ref, y_ref)):
            product = lax.dot_general(
                left[:, first:after], x_ref[:, first:], dims, preferred_element_type=jnp.float32
            )
            product = (product * (1.0 / SPECTRA)).astype(jnp.bfloat16)
            result[part, first:after, first:] = product
            if after < SIGNALS:
                mirror = product[:, BLOCK:].T
                result[part, after:, first:after] = mirror if part == 0 else -mirror
        if out_ref is None:
            continue
        rows = pl.ds(first, BLOCK)
        copy = pltpu.make_async_copy(result.at[:, rows], out_ref.at[:, rows], sem.at[step])
        copy.start()
        copies.append(copy)
    return copies


def spread(
    volt_ref, taps_ref, table_ref, result, x_ref, y_ref,
    frames, weights, filtered, main, tails, outbox, outbox_late, inbox, inbox_late, lifted, added,
    near_sem, pair_sem, send_sem, recv_sem,
):
    row, col = lax.axis_index("row"), lax.axis_index("col")
    me = row * 16 + col
    core = col % 2
    barrier = pltpu.get_barrier_semaphore()
    for offset in ORDER:
        pl.semaphore_signal(barrier, inc=1, device_id=partner(offset), device_id_type=MESH)

    near = pltpu.make_async_copy(volt_ref, frames.at[pl.ds(LATE * POINTS, OWN * POINTS)], near_sem)
    near.start()
    padded = jnp.concatenate([taps_ref[...], jnp.zeros((LANES - TAPS, POINTS), jnp.float32)], axis=0)
    for first in range(0, POINTS, LANES):
        columns = padded[:, first : first + LANES].T
        for tap in range(TAPS):
            weights[tap, first : first + LANES, :] = jnp.broadcast_to(columns[:, tap : tap + 1], (LANES, LANES))
    added[...] = jnp.zeros(added.shape, jnp.float32)
    halo = pltpu.make_async_remote_copy(
        src_ref=volt_ref.at[pl.ds((OWN - LATE) * POINTS, LATE * POINTS)],
        dst_ref=frames.at[pl.ds(0, LATE * POINTS)],
        send_sem=pair_sem.at[0],
        recv_sem=pair_sem.at[1],
        device_id=partner((0, 0, 0, 1)),
        device_id_type=MESH,
    )

    def filter_frames(outputs, slots):
        def rows16(step, carry):
            rows = pl.ds(pl.multiple_of(step * 16, 16), 16)
            taps = [jnp.concatenate([weights[tap, rows, :]] * 2, axis=1) for tap in range(TAPS)]
            for left in range(0, SIGNALS, 256):
                lanes = slice(left, left + 256)
                values = {}
                for slot in slots:
                    at = pl.ds(pl.multiple_of(slot * POINTS + step * 16, 16), 16)
                    values[slot] = frames[at, lanes].astype(jnp.float32)
                for frame in outputs:
                    total = None
                    for tap in range(TAPS):
                        if frame + tap in values:
                            term = taps[tap] * values[frame + tap]
                            total = term if total is None else total + term
                    filtered[frame, rows, lanes] = total.astype(jnp.bfloat16)
            return carry

        lax.fori_loop(0, POINTS // 16, rows16, 0)

    def transform(channel, index, frame):
        half = index % 2
        lanes = pl.ds(pl.multiple_of(half * HALF, HALF), HALF)
        return half, jnp.dot(table_ref[channel], filtered[frame, :, lanes], preferred_element_type=jnp.float32)

    def transform_main(channel):
        def one(index, carry):
            frame = index // 2
            half, spectrum = transform(channel, index, frame)
            for group in range(GROUPS // 2):
                rows = pl.ds(frame, 2 * DEVICES, stride=OWN)
                main[half * (GROUPS // 2) + group, rows, :] = spectrum[:, group * LANES : (group + 1) * LANES]
            return carry

        lax.fori_loop(0, 2 * OWN, one, 0)

    def transform_late(channel):
        def one(index, carry):
            late = index // 2
            half, spectrum = transform(channel, index, late + OWN)
            for group in range(GROUPS // 2):
                rows = pl.ds(half * (GROUPS // 2) + group, 2 * DEVICES, stride=GROUPS)
                tails[late, rows, :] = spectrum[:, group * LANES : (group + 1) * LANES]
            return carry

        lax.fori_loop(0, 2 * LATE, one, 0)

    def pack_main(channel):
        def one(target, carry):
            rows = pl.ds(pl.multiple_of(target * 8, 8), 8)
            for group in range(GROUPS // 2):
                both = jnp.concatenate([main[group, rows, :], main[group + GROUPS // 2, rows, :]], axis=0)
                outbox[channel, target, :, group * LANES : (group + 1) * LANES] = both.astype(jnp.bfloat16)
            return carry

        lax.fori_loop(0, DEVICES, one, 0, unroll=4)

    def pack_late(channel):
        def one(target, carry):
            rows = pl.ds(pl.multiple_of(target * 16, 16), 16)
            for late in range(LATE):
                outbox_late[channel, target, :, late * LANES : (late + 1) * LANES] = tails[late, rows, :].astype(
                    jnp.bfloat16
                )
            return carry

        lax.fori_loop(0, DEVICES, one, 0, unroll=4)

    def send(channel, box, into, place, sem):
        for offset in ORDER:
            to = partner(offset)
            pltpu.make_async_remote_copy(
                src_ref=box.at[channel, to[0] * 16 + to[1]],
                dst_ref=into.at[channel, place],
                send_sem=send_sem.at[sem],
                recv_sem=recv_sem.at[sem],
                device_id=to,
                device_id_type=MESH,
            ).start()

    def arrived(channel):
        most = inbox.at[channel, pl.ds(0, DEVICES - 1)]
        pltpu.make_async_copy(most, most, recv_sem.at[channel]).wait()

        @pl.when(core == 0)
        def _():
            late = inbox_late.at[channel]
            pltpu.make_async_copy(late, late, recv_sem.at[2 + channel]).wait()

        @pl.when(core == 1)
        def _():
            late = inbox_late.at[channel, pl.ds(0, DEVICES // 2 - 1)]
            pltpu.make_async_copy(late, late, recv_sem.at[2 + channel]).wait()

    def merge(channel):
        row_of = lax.broadcasted_iota(jnp.int32, (16, LANES), 0)
        sign = jnp.where(row_of % 8 < OWN, 1.0, -1.0).astype(jnp.float32)

        def eight(step, carry):
            first = step * 8
            for index in range(8):
                chip = first + index
                before = jnp.maximum(chip - 1, 0)
                for late in range(LATE):
                    tail = inbox_late[channel, before, :, late * LANES : (late + 1) * LANES].astype(jnp.float32)
                    lifted[late, index * 16 : (index + 1) * 16, :] = jnp.where(chip > 0, tail, 0.0)
            for late in range(LATE):
                for group in range(GROUPS):
                    added[group, pl.ds(late, 16, stride=OWN), :] = lifted[late, pl.ds(group, 16, stride=GROUPS), :]
            for index in range(8):
                chip = first + index
                rows = pl.ds(pl.multiple_of(chip * 16, 16), 16)
                for group in range(GROUPS // 2):
                    lanes = slice(group * LANES, (group + 1) * LANES)
                    lower = inbox[channel, 2 * chip, :, lanes].astype(jnp.float32)
                    upper = inbox[channel, 2 * chip + 1, :, lanes].astype(jnp.float32)
                    for half in range(2):
                        whole = half * (GROUPS // 2) + group
                        extra = added[whole, index * 8 : index * 8 + 8, :]
                        part = slice(half * 8, half * 8 + 8)
                        early = lower[part] + extra
                        value = jnp.concatenate([early, upper[part]], axis=0)
                        turned = jnp.concatenate(
                            [pltpu.roll(early, OWN, 0), pltpu.roll(upper[part], OWN, 0)], axis=0
                        )
                        out = slice(whole * LANES, (whole + 1) * LANES)
                        x_ref[rows, out] = value.astype(jnp.bfloat16)
                        y_ref[rows, out] = (turned * sign).astype(jnp.bfloat16)
            return carry

        lax.fori_loop(0, DEVICES // 16, eight, 0)

    near.wait()

    @pl.when(core == 0)
    def _():
        frames[0 : LATE * POINTS, :] = jnp.zeros((LATE * POINTS, SIGNALS), jnp.bfloat16)
        filter_frames(range(OWN), range(OWN + LATE))
        transform_main(0)
        pack_main(0)
        pl.semaphore_wait(barrier, len(ORDER))
        halo.start()
        send(0, outbox, inbox, me, 0)

    @pl.when(core == 1)
    def _():
        filter_frames(range(OWN, OWN + LATE), range(OWN, OWN + LATE))
        transform_late(0)
        pack_late(0)
        pl.semaphore_wait(barrier, len(ORDER))
        send(0, outbox_late, inbox_late, me // 2, 2)
        inbox_late[0, me // 2] = outbox_late[0, me]
        halo.wait_recv()
        filter_frames(range(OWN), range(OWN + LATE))
        transform_main(0)
        pack_main(0)
        send(0, outbox, inbox, me, 0)
        transform_late(1)
        pack_late(1)
        send(1, outbox_late, inbox_late, me // 2, 3)
        inbox_late[1, me // 2] = outbox_late[1, me]

    inbox[0, me] = outbox[0, me]
    transform_main(1)
    pack_main(1)
    send(1, outbox, inbox, me, 1)
    inbox[1, me] = outbox[1, me]

    arrived(0)
    merge(0)
    correlate(x_ref, y_ref, result)
    arrived(1)
    merge(1)
    for channel in range(2):
        most = outbox.at[channel, pl.ds(0, DEVICES - 1)]
        pltpu.make_async_copy(most, most, send_sem.at[channel]).wait()

    @pl.when(core == 0)
    def _():
        halo.wait_send()

    @pl.when(core == 1)
    def _():
        for channel in range(2):
            most = outbox_late.at[channel, pl.ds(0, DEVICES - 1)]
            pltpu.make_async_copy(most, most, send_sem.at[2 + channel]).wait()


def finish(vis_ref, x_ref, y_ref, out_ref, result, done_sem, out_sem):
    done = pltpu.make_async_copy(vis_ref, out_ref.at[0], done_sem)
    done.start()
    for copy in correlate(x_ref, y_ref, result, out_ref.at[1], out_sem):
        copy.wait()
    done.wait()


def shards(voltages, filter_taps):
    inputs = voltages.shape[1]
    vmem = pl.BlockSpec(memory_space=pltpu.VMEM)
    anywhere = pl.BlockSpec(memory_space=pl.ANY)
    bf16, f32 = jnp.bfloat16, jnp.float32
    square = pltpu.VMEM((2 * SPECTRA, inputs), bf16)
    kept = [pltpu.VMEM((2, inputs, inputs), bf16), square, square]
    kept = pl.pallas_call(
        spread,
        name="spread",
        out_shape=kept,
        in_specs=[anywhere, vmem, vmem],
        out_specs=[vmem] * 3,
        scratch_shapes=[
            pltpu.VMEM(((OWN + LATE) * POINTS, SIGNALS), bf16),
            pltpu.VMEM((TAPS, POINTS, LANES), f32),
            pltpu.VMEM((OWN + LATE, POINTS, SIGNALS), bf16),
            pltpu.VMEM((GROUPS, DEVICES * 2 * OWN, LANES), f32),
            pltpu.VMEM((LATE, DEVICES * 2 * GROUPS, LANES), f32),
            pltpu.VMEM((2, DEVICES, 16, HALF), bf16),
            pltpu.VMEM((2, DEVICES, 16, LATE * LANES), bf16),
            pltpu.VMEM((2, DEVICES, 16, HALF), bf16),
            pltpu.VMEM((2, DEVICES // 2, 16, LATE * LANES), bf16),
            pltpu.VMEM((LATE, 128, LANES), f32),
            pltpu.VMEM((GROUPS, 64, LANES), f32),
            pltpu.SemaphoreType.DMA(()),
            pltpu.SemaphoreType.DMA((2,)),
            pltpu.SemaphoreType.DMA((4,)),
            pltpu.SemaphoreType.DMA((4,)),
        ],
        compiler_params=pltpu.CompilerParams(
            collective_id=0, has_side_effects=True, vmem_limit_bytes=50 << 20
        ),
    )(voltages, filter_taps, jnp.asarray(fourier_rows()))
    kept = [pltpu.with_memory_space_constraint(array, pltpu.VMEM) for array in kept]
    return pl.pallas_call(
        finish,
        name="finish",
        out_shape=jax.ShapeDtypeStruct((2, 2, inputs, inputs), bf16),
        in_specs=[vmem] * 3,
        out_specs=anywhere,
        scratch_shapes=[
            pltpu.VMEM((2, SIGNALS, SIGNALS), bf16),
            pltpu.SemaphoreType.DMA(()),
            pltpu.SemaphoreType.DMA((SIGNALS // BLOCK,)),
        ],
        compiler_params=pltpu.CompilerParams(vmem_limit_bytes=48 << 20),
    )(*kept)


def solution(mesh):
    placed = (P(("row", "col"), None), P())
    return jax.shard_map(
        shards,
        mesh=mesh,
        in_specs=placed,
        out_specs=P(("row", "col"), None, None, None),
        check_vma=False,
    )
```

```python
import itertools

import jax
import jax.numpy as jnp
import numpy as np
from jax import lax
from jax.experimental import pallas as pl
from jax.experimental.pallas import tpu as pltpu
from jax.sharding import PartitionSpec as P

MESH = pl.DeviceIdType.MESH
DEVICES = 128
POINTS = 512
TAPS = 4
SPECTRA = 512
OWN = 4
LATE = TAPS - 1
SIGNALS = 1024
HALF = SIGNALS // 2
LANES = 128
GROUPS = SIGNALS // LANES
BLOCK = 256
STARTS = (0, 1024, 1792, 2304, 2560)


def orbit(offset):
    found = set()
    for turn in range(3):
        turned = offset[turn:] + offset[:turn]
        found.add(turned)
        found.add(tuple((-step) % 4 for step in turned))
    return tuple(sorted(found))


def send_order():
    hops = lambda group: sum(min(step, 4 - step) for step in group[0])
    groups = {orbit(offset) for offset in itertools.product(range(4), repeat=3)}
    ordered = []
    for group in sorted(sorted(groups), key=hops, reverse=True):
        for core in (0, 1):
            ordered += [offset + (core,) for offset in group]
    return [offset for offset in ordered if any(offset)]


ORDER = send_order()
ODD = [offset for offset in ORDER if offset[1] % 2 == 1]
EVEN = [offset for offset in ORDER if offset[1] % 2 == 0]


def coordinates():
    row, col = lax.axis_index("row"), lax.axis_index("col")
    return ((col // 2) % 2) * 2 + row // 4, row % 4, col // 4, col % 2


def partner(offset):
    place = coordinates()
    x, y, z = ((own + step) % 4 for own, step in zip(place[:3], offset[:3]))
    core = (place[3] + offset[3]) % 2
    return (x % 2) * 4 + y, z * 4 + (x // 2) * 2 + core


def fourier_rows():
    turns = np.arange(POINTS // 2)[:, None] * np.arange(POINTS)[None, :] % POINTS
    phase = turns.astype(np.float32) * np.float32(2.0 * np.pi / POINTS)
    scale = np.float32(1.0) / np.sqrt(np.float32(POINTS))
    table = np.stack([np.cos(phase), -np.sin(phase)], axis=1) * scale
    table = table.reshape(DEVICES, 2, 2, POINTS).transpose(1, 0, 2, 3)
    return table.reshape(2, POINTS // 2, POINTS).astype(jnp.bfloat16)


def correlate(x_ref, y_ref, depth, result, base=None, out_ref=None, sem=None):
    copies = []
    for step in range(SIGNALS // BLOCK):
        first, after = step * BLOCK, (step + 1) * BLOCK
        for part in range(2):
            product = block_row(x_ref, y_ref, depth, step, part)
            if base is not None:
                product = product + base[part, :, STARTS[step] : STARTS[step + 1]]
            product = (product * (1.0 / SPECTRA)).astype(jnp.bfloat16)
            result[part, first:after, first:] = product
            if after < SIGNALS:
                mirror = product[:, BLOCK:].T
                result[part, after:, first:after] = mirror if part == 0 else -mirror
        if out_ref is None:
            continue
        rows = pl.ds(first, BLOCK)
        copy = pltpu.make_async_copy(result.at[:, rows], out_ref.at[:, rows], sem.at[step])
        copy.start()
        copies.append(copy)
    return copies


def block_row(x_ref, y_ref, depth, step, part):
    left = y_ref if part else x_ref
    return lax.dot_general(
        left[0:depth, step * BLOCK : (step + 1) * BLOCK],
        x_ref[0:depth, step * BLOCK :],
        (((0,), (0,)), ((), ())),
        preferred_element_type=jnp.float32,
    )


def spread(
    volt_ref, taps_ref, table_ref, result, sums, x_last, y_last,
    frames, weights, filtered, main, tails, outbox, outbox_late, inbox, inbox_late, lifted, added, x_ref, y_ref,
    near_sem, pair_sem, send_sem, recv_sem,
):
    row, col = lax.axis_index("row"), lax.axis_index("col")
    me = row * 16 + col
    core = col % 2
    barrier = pltpu.get_barrier_semaphore()
    for offset in ORDER:
        pl.semaphore_signal(barrier, inc=1, device_id=partner(offset), device_id_type=MESH)

    near = pltpu.make_async_copy(volt_ref, frames.at[pl.ds(LATE * POINTS, OWN * POINTS)], near_sem)
    near.start()
    padded = jnp.concatenate([taps_ref[...], jnp.zeros((LANES - TAPS, POINTS), jnp.float32)], axis=0)
    for first in range(0, POINTS, LANES):
        columns = padded[:, first : first + LANES].T
        for tap in range(TAPS):
            weights[tap, first : first + LANES, :] = jnp.broadcast_to(columns[:, tap : tap + 1], (LANES, LANES))
    added[...] = jnp.zeros(added.shape, jnp.float32)
    halo = pltpu.make_async_remote_copy(
        src_ref=volt_ref.at[pl.ds((OWN - LATE) * POINTS, LATE * POINTS)],
        dst_ref=frames.at[pl.ds(0, LATE * POINTS)],
        send_sem=pair_sem.at[0],
        recv_sem=pair_sem.at[1],
        device_id=partner((0, 0, 0, 1)),
        device_id_type=MESH,
    )

    def filter_frames(outputs, slots):
        def rows16(step, carry):
            rows = pl.ds(pl.multiple_of(step * 16, 16), 16)
            taps = [jnp.concatenate([weights[tap, rows, :]] * 2, axis=1) for tap in range(TAPS)]
            for left in range(0, SIGNALS, 256):
                lanes = slice(left, left + 256)
                values = {}
                for slot in slots:
                    at = pl.ds(pl.multiple_of(slot * POINTS + step * 16, 16), 16)
                    values[slot] = frames[at, lanes].astype(jnp.float32)
                for frame in outputs:
                    total = None
                    for tap in range(TAPS):
                        if frame + tap in values:
                            term = taps[tap] * values[frame + tap]
                            total = term if total is None else total + term
                    filtered[frame, rows, lanes] = total.astype(jnp.bfloat16)
            return carry

        lax.fori_loop(0, POINTS // 16, rows16, 0)

    def transform(channel, index, frame):
        half = index % 2
        lanes = pl.ds(pl.multiple_of(half * HALF, HALF), HALF)
        return half, jnp.dot(table_ref[channel], filtered[frame, :, lanes], preferred_element_type=jnp.float32)

    def transform_main(channel):
        def one(index, carry):
            frame = index // 2
            half, spectrum = transform(channel, index, frame)
            for group in range(GROUPS // 2):
                rows = pl.ds(frame, 2 * DEVICES, stride=OWN)
                main[half * (GROUPS // 2) + group, rows, :] = spectrum[:, group * LANES : (group + 1) * LANES]
            return carry

        lax.fori_loop(0, 2 * OWN, one, 0)

    def transform_late(channel):
        def one(index, carry):
            late = index // 2
            half, spectrum = transform(channel, index, late + OWN)
            for group in range(GROUPS // 2):
                rows = pl.ds(half * (GROUPS // 2) + group, 2 * DEVICES, stride=GROUPS)
                tails[late, rows, :] = spectrum[:, group * LANES : (group + 1) * LANES]
            return carry

        lax.fori_loop(0, 2 * LATE, one, 0)

    def pack_main(channel):
        def one(target, carry):
            rows = pl.ds(pl.multiple_of(target * 8, 8), 8)
            for group in range(GROUPS // 2):
                both = jnp.concatenate([main[group, rows, :], main[group + GROUPS // 2, rows, :]], axis=0)
                outbox[channel, target, :, group * LANES : (group + 1) * LANES] = both.astype(jnp.bfloat16)
            return carry

        lax.fori_loop(0, DEVICES, one, 0, unroll=4)

    def pack_late(channel):
        def one(target, carry):
            rows = pl.ds(pl.multiple_of(target * 16, 16), 16)
            for late in range(LATE):
                outbox_late[channel, target, :, late * LANES : (late + 1) * LANES] = tails[late, rows, :].astype(
                    jnp.bfloat16
                )
            return carry

        lax.fori_loop(0, DEVICES, one, 0, unroll=4)

    def send(channel, box, into, place, sem, order=ORDER):
        for offset in order:
            to = partner(offset)
            pltpu.make_async_remote_copy(
                src_ref=box.at[channel, to[0] * 16 + to[1]],
                dst_ref=into.at[channel, place],
                send_sem=send_sem.at[sem],
                recv_sem=recv_sem.at[sem],
                device_id=to,
                device_id_type=MESH,
            ).start()

    def arrived(channel, count, sem):
        most = inbox.at[channel, pl.ds(0, count)]
        pltpu.make_async_copy(most, most, recv_sem.at[sem]).wait()

    def arrived_late(channel):
        @pl.when(core == 0)
        def _():
            late = inbox_late.at[channel]
            pltpu.make_async_copy(late, late, recv_sem.at[2 + channel]).wait()

        @pl.when(core == 1)
        def _():
            late = inbox_late.at[channel, pl.ds(0, DEVICES // 2 - 1)]
            pltpu.make_async_copy(late, late, recv_sem.at[2 + channel]).wait()

    def merge(channel, count, chunk, x_to, y_to):
        row_of = lax.broadcasted_iota(jnp.int32, (16, LANES), 0)
        sign = jnp.where(row_of % 8 < OWN, 1.0, -1.0).astype(jnp.float32)

        def eight(step, carry):
            first = chunk(step) * 8
            for index in range(8):
                chip = first + index
                before = jnp.maximum(chip - 1, 0)
                for late in range(LATE):
                    tail = inbox_late[channel, before, :, late * LANES : (late + 1) * LANES].astype(jnp.float32)
                    lifted[late, index * 16 : (index + 1) * 16, :] = jnp.where(chip > 0, tail, 0.0)
            for late in range(LATE):
                for group in range(GROUPS):
                    added[group, pl.ds(late, 16, stride=OWN), :] = lifted[late, pl.ds(group, 16, stride=GROUPS), :]
            for index in range(8):
                chip = first + index
                rows = pl.ds(pl.multiple_of((step * 8 + index) * 16, 16), 16)
                for group in range(GROUPS // 2):
                    lanes = slice(group * LANES, (group + 1) * LANES)
                    lower = inbox[channel, 2 * chip, :, lanes].astype(jnp.float32)
                    upper = inbox[channel, 2 * chip + 1, :, lanes].astype(jnp.float32)
                    for half in range(2):
                        whole = half * (GROUPS // 2) + group
                        extra = added[whole, index * 8 : index * 8 + 8, :]
                        part = slice(half * 8, half * 8 + 8)
                        early = lower[part] + extra
                        value = jnp.concatenate([early, upper[part]], axis=0)
                        turned = jnp.concatenate(
                            [pltpu.roll(early, OWN, 0), pltpu.roll(upper[part], OWN, 0)], axis=0
                        )
                        out = slice(whole * LANES, (whole + 1) * LANES)
                        x_to[rows, out] = value.astype(jnp.bfloat16)
                        y_to[rows, out] = (turned * sign).astype(jnp.bfloat16)
            return carry

        lax.fori_loop(0, count, eight, 0)

    near.wait()

    @pl.when(core == 0)
    def _():
        frames[0 : LATE * POINTS, :] = jnp.zeros((LATE * POINTS, SIGNALS), jnp.bfloat16)
        filter_frames(range(OWN), range(OWN + LATE))
        transform_main(0)
        pack_main(0)
        pl.semaphore_wait(barrier, len(ORDER))
        halo.start()
        send(0, outbox, inbox, me, 0)

    @pl.when(core == 1)
    def _():
        filter_frames(range(OWN, OWN + LATE), range(OWN, OWN + LATE))
        transform_late(0)
        pack_late(0)
        pl.semaphore_wait(barrier, len(ORDER))
        send(0, outbox_late, inbox_late, me // 2, 2)
        inbox_late[0, me // 2] = outbox_late[0, me]
        halo.wait_recv()
        filter_frames(range(OWN), range(OWN + LATE))
        transform_main(0)
        pack_main(0)
        send(0, outbox, inbox, me, 0)
        transform_late(1)
        pack_late(1)
        send(1, outbox_late, inbox_late, me // 2, 3)
        inbox_late[1, me // 2] = outbox_late[1, me]

    inbox[0, me] = outbox[0, me]
    transform_main(1)
    pack_main(1)
    send(1, outbox, inbox, me, 1, ODD)
    send(1, outbox, inbox, me, 4, EVEN)
    inbox[1, me] = outbox[1, me]

    y = row % 4
    arrived(0, DEVICES - 1, 0)
    arrived_late(0)
    merge(0, 8, lambda step: step, x_ref, y_ref)
    correlate(x_ref, y_ref, 2 * SPECTRA, result)
    arrived_late(1)
    arrived(1, len(ODD), 1)
    merge(1, 4, lambda step: step // 2 * 4 + (y + 1 + step % 2 * 2) % 4, x_ref, y_ref)
    for step in range(SIGNALS // BLOCK):
        for part in range(2):
            sums[part, :, STARTS[step] : STARTS[step + 1]] = block_row(x_ref, y_ref, SPECTRA, step, part)
    arrived(1, len(EVEN), 4)
    merge(1, 4, lambda step: step // 2 * 4 + (y + step % 2 * 2) % 4, x_last, y_last)
    for channel, count, sem in ((0, DEVICES - 1, 0), (1, len(ODD), 1), (1, len(EVEN), 4)):
        most = outbox.at[channel, pl.ds(0, count)]
        pltpu.make_async_copy(most, most, send_sem.at[sem]).wait()

    @pl.when(core == 0)
    def _():
        halo.wait_send()

    @pl.when(core == 1)
    def _():
        for channel in range(2):
            most = outbox_late.at[channel, pl.ds(0, DEVICES - 1)]
            pltpu.make_async_copy(most, most, send_sem.at[2 + channel]).wait()


def finish(vis_ref, sums, x_ref, y_ref, out_ref, result, done_sem, out_sem):
    done = pltpu.make_async_copy(vis_ref, out_ref.at[0], done_sem)
    done.start()
    for copy in correlate(x_ref, y_ref, SPECTRA, result, sums, out_ref.at[1], out_sem):
        copy.wait()
    done.wait()


def shards(voltages, filter_taps):
    inputs = voltages.shape[1]
    vmem = pl.BlockSpec(memory_space=pltpu.VMEM)
    anywhere = pl.BlockSpec(memory_space=pl.ANY)
    bf16, f32 = jnp.bfloat16, jnp.float32
    last = pltpu.VMEM((SPECTRA, inputs), bf16)
    kept = [pltpu.VMEM((2, inputs, inputs), bf16), pltpu.VMEM((2, BLOCK, STARTS[-1]), f32), last, last]
    kept = pl.pallas_call(
        spread,
        name="spread",
        out_shape=kept,
        in_specs=[anywhere, vmem, vmem],
        out_specs=[vmem] * 4,
        scratch_shapes=[
            pltpu.VMEM(((OWN + LATE) * POINTS, SIGNALS), bf16),
            pltpu.VMEM((TAPS, POINTS, LANES), f32),
            pltpu.VMEM((OWN + LATE, POINTS, SIGNALS), bf16),
            pltpu.VMEM((GROUPS, DEVICES * 2 * OWN, LANES), f32),
            pltpu.VMEM((LATE, DEVICES * 2 * GROUPS, LANES), f32),
            pltpu.VMEM((2, DEVICES, 16, HALF), bf16),
            pltpu.VMEM((2, DEVICES, 16, LATE * LANES), bf16),
            pltpu.VMEM((2, DEVICES, 16, HALF), bf16),
            pltpu.VMEM((2, DEVICES // 2, 16, LATE * LANES), bf16),
            pltpu.VMEM((LATE, 128, LANES), f32),
            pltpu.VMEM((GROUPS, 64, LANES), f32),
            pltpu.VMEM((2 * SPECTRA, SIGNALS), bf16),
            pltpu.VMEM((2 * SPECTRA, SIGNALS), bf16),
            pltpu.SemaphoreType.DMA(()),
            pltpu.SemaphoreType.DMA((2,)),
            pltpu.SemaphoreType.DMA((5,)),
            pltpu.SemaphoreType.DMA((5,)),
        ],
        compiler_params=pltpu.CompilerParams(
            collective_id=0, has_side_effects=True, vmem_limit_bytes=48 << 20
        ),
    )(voltages, filter_taps, jnp.asarray(fourier_rows()))
    kept = [pltpu.with_memory_space_constraint(array, pltpu.VMEM) for array in kept]
    return pl.pallas_call(
        finish,
        name="finish",
        out_shape=jax.ShapeDtypeStruct((2, 2, inputs, inputs), bf16),
        in_specs=[vmem] * 4,
        out_specs=anywhere,
        scratch_shapes=[
            pltpu.VMEM((2, SIGNALS, SIGNALS), bf16),
            pltpu.SemaphoreType.DMA(()),
            pltpu.SemaphoreType.DMA((SIGNALS // BLOCK,)),
        ],
        compiler_params=pltpu.CompilerParams(vmem_limit_bytes=48 << 20),
    )(*kept)


def solution(mesh):
    placed = (P(("row", "col"), None), P())
    return jax.shard_map(
        shards,
        mesh=mesh,
        in_specs=placed,
        out_specs=P(("row", "col"), None, None, None),
        check_vma=False,
    )
```

```python
import itertools

import jax
import jax.numpy as jnp
import numpy as np
from jax import lax
from jax.experimental import pallas as pl
from jax.experimental.pallas import tpu as pltpu
from jax.sharding import PartitionSpec as P

MESH = pl.DeviceIdType.MESH
DEVICES = 128
POINTS = 512
TAPS = 4
SPECTRA = 512
OWN = 4
LATE = TAPS - 1
SIGNALS = 1024
HALF = SIGNALS // 2
LANES = 128
GROUPS = SIGNALS // LANES
BLOCK = 256
STARTS = (0, 1024, 1792, 2304, 2560)


def orbit(offset):
    found = set()
    for turn in range(3):
        turned = offset[turn:] + offset[:turn]
        found.add(turned)
        found.add(tuple((-step) % 4 for step in turned))
    return tuple(sorted(found))


def send_order():
    hops = lambda group: sum(min(step, 4 - step) for step in group[0])
    groups = {orbit(offset) for offset in itertools.product(range(4), repeat=3)}
    ordered = []
    for group in sorted(sorted(groups), key=hops, reverse=True):
        for core in (0, 1):
            ordered += [offset + (core,) for offset in group]
    return [offset for offset in ordered if any(offset)]


ORDER = send_order()
CHIPS = list(dict.fromkeys(offset[:3] for offset in ORDER))
EDGES = (0, 22, 51, 64)
LOTS = [CHIPS[first:last] for first, last in zip(EDGES, EDGES[1:])]
SENDS = [[offset for offset in ORDER if offset[:3] in lot] for lot in LOTS]
LOT_SEM = (1, 4, 5)
LAST = 16 * len(LOTS[-1])


def coordinates():
    row, col = lax.axis_index("row"), lax.axis_index("col")
    return ((col // 2) % 2) * 2 + row // 4, row % 4, col // 4, col % 2


def partner(offset):
    place = coordinates()
    x, y, z = ((own + step) % 4 for own, step in zip(place[:3], offset[:3]))
    core = (place[3] + offset[3]) % 2
    return (x % 2) * 4 + y, z * 4 + (x // 2) * 2 + core


def fourier_rows():
    turns = np.arange(POINTS // 2)[:, None] * np.arange(POINTS)[None, :] % POINTS
    phase = turns.astype(np.float32) * np.float32(2.0 * np.pi / POINTS)
    scale = np.float32(1.0) / np.sqrt(np.float32(POINTS))
    table = np.stack([np.cos(phase), -np.sin(phase)], axis=1) * scale
    table = table.reshape(DEVICES, 2, 2, POINTS).transpose(1, 0, 2, 3)
    return table.reshape(2, POINTS // 2, POINTS).astype(jnp.bfloat16)


def correlate(x_ref, y_ref, depth, result, base=None, out_ref=None, sem=None):
    copies = []
    for step in range(SIGNALS // BLOCK):
        first, after = step * BLOCK, (step + 1) * BLOCK
        for part in range(2):
            product = block_row(x_ref, y_ref, depth, step, part)
            if base is not None:
                product = product + base[part, :, STARTS[step] : STARTS[step + 1]]
            product = (product * (1.0 / SPECTRA)).astype(jnp.bfloat16)
            result[part, first:after, first:] = product
            if after < SIGNALS:
                mirror = product[:, BLOCK:].T
                result[part, after:, first:after] = mirror if part == 0 else -mirror
        if out_ref is None:
            continue
        rows = pl.ds(first, BLOCK)
        copy = pltpu.make_async_copy(result.at[:, rows], out_ref.at[:, rows], sem.at[step])
        copy.start()
        copies.append(copy)
    return copies


def block_row(x_ref, y_ref, depth, step, part):
    left = y_ref if part else x_ref
    return lax.dot_general(
        left[0:depth, step * BLOCK : (step + 1) * BLOCK],
        x_ref[0:depth, step * BLOCK :],
        (((0,), (0,)), ((), ())),
        preferred_element_type=jnp.float32,
    )


def spread(
    volt_ref, taps_ref, table_ref, result, sums, x_last, y_last,
    frames, weights, filtered, main, tails, outbox, outbox_late, inbox, inbox_late, lifted, added, x_ref, y_ref,
    near_sem, pair_sem, send_sem, recv_sem,
):
    row, col = lax.axis_index("row"), lax.axis_index("col")
    me = row * 16 + col
    core = col % 2
    barrier = pltpu.get_barrier_semaphore()
    for offset in ORDER:
        pl.semaphore_signal(barrier, inc=1, device_id=partner(offset), device_id_type=MESH)

    near = pltpu.make_async_copy(volt_ref, frames.at[pl.ds(LATE * POINTS, OWN * POINTS)], near_sem)
    near.start()
    padded = jnp.concatenate([taps_ref[...], jnp.zeros((LANES - TAPS, POINTS), jnp.float32)], axis=0)
    for first in range(0, POINTS, LANES):
        columns = padded[:, first : first + LANES].T
        for tap in range(TAPS):
            weights[tap, first : first + LANES, :] = jnp.broadcast_to(columns[:, tap : tap + 1], (LANES, LANES))
    added[...] = jnp.zeros(added.shape, jnp.float32)
    halo = pltpu.make_async_remote_copy(
        src_ref=volt_ref.at[pl.ds((OWN - LATE) * POINTS, LATE * POINTS)],
        dst_ref=frames.at[pl.ds(0, LATE * POINTS)],
        send_sem=pair_sem.at[0],
        recv_sem=pair_sem.at[1],
        device_id=partner((0, 0, 0, 1)),
        device_id_type=MESH,
    )

    def filter_frames(outputs, slots):
        def rows16(step, carry):
            rows = pl.ds(pl.multiple_of(step * 16, 16), 16)
            taps = [jnp.concatenate([weights[tap, rows, :]] * 2, axis=1) for tap in range(TAPS)]
            for left in range(0, SIGNALS, 256):
                lanes = slice(left, left + 256)
                values = {}
                for slot in slots:
                    at = pl.ds(pl.multiple_of(slot * POINTS + step * 16, 16), 16)
                    values[slot] = frames[at, lanes].astype(jnp.float32)
                for frame in outputs:
                    total = None
                    for tap in range(TAPS):
                        if frame + tap in values:
                            term = taps[tap] * values[frame + tap]
                            total = term if total is None else total + term
                    filtered[frame, rows, lanes] = total.astype(jnp.bfloat16)
            return carry

        lax.fori_loop(0, POINTS // 16, rows16, 0)

    def transform(channel, index, frame):
        half = index % 2
        lanes = pl.ds(pl.multiple_of(half * HALF, HALF), HALF)
        return half, jnp.dot(table_ref[channel], filtered[frame, :, lanes], preferred_element_type=jnp.float32)

    def transform_main(channel):
        def one(index, carry):
            frame = index // 2
            half, spectrum = transform(channel, index, frame)
            for group in range(GROUPS // 2):
                rows = pl.ds(frame, 2 * DEVICES, stride=OWN)
                main[half * (GROUPS // 2) + group, rows, :] = spectrum[:, group * LANES : (group + 1) * LANES]
            return carry

        lax.fori_loop(0, 2 * OWN, one, 0)

    def transform_late(channel):
        def one(index, carry):
            late = index // 2
            half, spectrum = transform(channel, index, late + OWN)
            for group in range(GROUPS // 2):
                rows = pl.ds(half * (GROUPS // 2) + group, 2 * DEVICES, stride=GROUPS)
                tails[late, rows, :] = spectrum[:, group * LANES : (group + 1) * LANES]
            return carry

        lax.fori_loop(0, 2 * LATE, one, 0)

    def pack_main(channel):
        def one(target, carry):
            rows = pl.ds(pl.multiple_of(target * 8, 8), 8)
            for group in range(GROUPS // 2):
                both = jnp.concatenate([main[group, rows, :], main[group + GROUPS // 2, rows, :]], axis=0)
                outbox[channel, target, :, group * LANES : (group + 1) * LANES] = both.astype(jnp.bfloat16)
            return carry

        lax.fori_loop(0, DEVICES, one, 0, unroll=4)

    def pack_late(channel):
        def one(target, carry):
            rows = pl.ds(pl.multiple_of(target * 16, 16), 16)
            for late in range(LATE):
                outbox_late[channel, target, :, late * LANES : (late + 1) * LANES] = tails[late, rows, :].astype(
                    jnp.bfloat16
                )
            return carry

        lax.fori_loop(0, DEVICES, one, 0, unroll=4)

    def send(channel, box, into, place, sem, order=ORDER):
        for offset in order:
            to = partner(offset)
            pltpu.make_async_remote_copy(
                src_ref=box.at[channel, to[0] * 16 + to[1]],
                dst_ref=into.at[channel, place],
                send_sem=send_sem.at[sem],
                recv_sem=recv_sem.at[sem],
                device_id=to,
                device_id_type=MESH,
            ).start()

    def arrived(channel, count, sem):
        most = inbox.at[channel, pl.ds(0, count)]
        pltpu.make_async_copy(most, most, recv_sem.at[sem]).wait()

    def arrived_late(channel):
        @pl.when(core == 0)
        def _():
            late = inbox_late.at[channel]
            pltpu.make_async_copy(late, late, recv_sem.at[2 + channel]).wait()

        @pl.when(core == 1)
        def _():
            late = inbox_late.at[channel, pl.ds(0, DEVICES // 2 - 1)]
            pltpu.make_async_copy(late, late, recv_sem.at[2 + channel]).wait()

    def lift(channel):
        def eight(step, carry):
            for index in range(8):
                chip = step * 8 + index
                before = jnp.maximum(chip - 1, 0)
                for late in range(LATE):
                    tail = inbox_late[channel, before, :, late * LANES : (late + 1) * LANES].astype(jnp.float32)
                    lifted[late, index * 16 : (index + 1) * 16, :] = jnp.where(chip > 0, tail, 0.0)
            for late in range(LATE):
                for group in range(GROUPS):
                    rows = pl.ds(step * 64 + late, 16, stride=OWN)
                    added[group, rows, :] = lifted[late, pl.ds(group, 16, stride=GROUPS), :]
            return carry

        lax.fori_loop(0, DEVICES // 16, eight, 0)

    def merge(channel, chip, rows, x_to, y_to):
        row_of = lax.broadcasted_iota(jnp.int32, (16, LANES), 0)
        sign = jnp.where(row_of % 8 < OWN, 1.0, -1.0).astype(jnp.float32)
        extra_rows = pl.ds(pl.multiple_of(chip * 8, 8), 8)
        for group in range(GROUPS // 2):
            lanes = slice(group * LANES, (group + 1) * LANES)
            lower = inbox[channel, 2 * chip, :, lanes].astype(jnp.float32)
            upper = inbox[channel, 2 * chip + 1, :, lanes].astype(jnp.float32)
            for half in range(2):
                whole = half * (GROUPS // 2) + group
                part = slice(half * 8, half * 8 + 8)
                early = lower[part] + added[whole, extra_rows, :]
                value = jnp.concatenate([early, upper[part]], axis=0)
                turned = jnp.concatenate([pltpu.roll(early, OWN, 0), pltpu.roll(upper[part], OWN, 0)], axis=0)
                out = slice(whole * LANES, (whole + 1) * LANES)
                x_to[rows, out] = value.astype(jnp.bfloat16)
                y_to[rows, out] = (turned * sign).astype(jnp.bfloat16)

    def merge_whole(channel):
        def eight(step, carry):
            for index in range(8):
                chip = step * 8 + index
                merge(channel, chip, pl.ds(pl.multiple_of(chip * 16, 16), 16), x_ref, y_ref)
            return carry

        lax.fori_loop(0, DEVICES // 16, eight, 0)

    def merge_lot(channel, lot, x_to, y_to):
        for index, offset in enumerate(LOTS[lot]):
            place = partner(offset + (0,))
            merge(channel, place[0] * 8 + place[1] // 2, slice(index * 16, index * 16 + 16), x_to, y_to)

    near.wait()

    @pl.when(core == 0)
    def _():
        frames[0 : LATE * POINTS, :] = jnp.zeros((LATE * POINTS, SIGNALS), jnp.bfloat16)
        filter_frames(range(OWN), range(OWN + LATE))
        transform_main(0)
        pack_main(0)
        pl.semaphore_wait(barrier, len(ORDER))
        halo.start()
        send(0, outbox, inbox, me, 0)

    @pl.when(core == 1)
    def _():
        filter_frames(range(OWN, OWN + LATE), range(OWN, OWN + LATE))
        transform_late(0)
        pack_late(0)
        pl.semaphore_wait(barrier, len(ORDER))
        send(0, outbox_late, inbox_late, me // 2, 2)
        inbox_late[0, me // 2] = outbox_late[0, me]
        halo.wait_recv()
        filter_frames(range(OWN), range(OWN + LATE))
        transform_main(0)
        pack_main(0)
        send(0, outbox, inbox, me, 0)
        transform_late(1)
        pack_late(1)
        send(1, outbox_late, inbox_late, me // 2, 3)
        inbox_late[1, me // 2] = outbox_late[1, me]

    inbox[0, me] = outbox[0, me]
    transform_main(1)
    pack_main(1)
    for sends, sem in zip(SENDS, LOT_SEM):
        send(1, outbox, inbox, me, sem, sends)
    inbox[1, me] = outbox[1, me]

    arrived(0, DEVICES - 1, 0)
    arrived_late(0)
    lift(0)
    merge_whole(0)
    correlate(x_ref, y_ref, 2 * SPECTRA, result)
    arrived_late(1)
    lift(1)
    for lot in range(len(LOTS) - 1):
        arrived(1, len(SENDS[lot]), LOT_SEM[lot])
        merge_lot(1, lot, x_ref, y_ref)
        for step in range(SIGNALS // BLOCK):
            columns = slice(STARTS[step], STARTS[step + 1])
            for part in range(2):
                product = block_row(x_ref, y_ref, 16 * len(LOTS[lot]), step, part)
                sums[part, :, columns] = product if lot == 0 else sums[part, :, columns] + product
    arrived(1, len(SENDS[-1]), LOT_SEM[-1])
    merge_lot(1, len(LOTS) - 1, x_last, y_last)
    for channel, count, sem in [(0, DEVICES - 1, 0)] + [(1, len(sends), sem) for sends, sem in zip(SENDS, LOT_SEM)]:
        most = outbox.at[channel, pl.ds(0, count)]
        pltpu.make_async_copy(most, most, send_sem.at[sem]).wait()

    @pl.when(core == 0)
    def _():
        halo.wait_send()

    @pl.when(core == 1)
    def _():
        for channel in range(2):
            most = outbox_late.at[channel, pl.ds(0, DEVICES - 1)]
            pltpu.make_async_copy(most, most, send_sem.at[2 + channel]).wait()


def finish(vis_ref, sums, x_ref, y_ref, out_ref, result, done_sem, out_sem):
    done = pltpu.make_async_copy(vis_ref, out_ref.at[0], done_sem)
    done.start()
    for copy in correlate(x_ref, y_ref, LAST, result, sums, out_ref.at[1], out_sem):
        copy.wait()
    done.wait()


def shards(voltages, filter_taps):
    inputs = voltages.shape[1]
    vmem = pl.BlockSpec(memory_space=pltpu.VMEM)
    anywhere = pl.BlockSpec(memory_space=pl.ANY)
    bf16, f32 = jnp.bfloat16, jnp.float32
    last = pltpu.VMEM((LAST, inputs), bf16)
    kept = [pltpu.VMEM((2, inputs, inputs), bf16), pltpu.VMEM((2, BLOCK, STARTS[-1]), f32), last, last]
    kept = pl.pallas_call(
        spread,
        name="spread",
        out_shape=kept,
        in_specs=[anywhere, vmem, vmem],
        out_specs=[vmem] * 4,
        scratch_shapes=[
            pltpu.VMEM(((OWN + LATE) * POINTS, SIGNALS), bf16),
            pltpu.VMEM((TAPS, POINTS, LANES), f32),
            pltpu.VMEM((OWN + LATE, POINTS, SIGNALS), bf16),
            pltpu.VMEM((GROUPS, DEVICES * 2 * OWN, LANES), f32),
            pltpu.VMEM((LATE, DEVICES * 2 * GROUPS, LANES), f32),
            pltpu.VMEM((2, DEVICES, 16, HALF), bf16),
            pltpu.VMEM((2, DEVICES, 16, LATE * LANES), bf16),
            pltpu.VMEM((2, DEVICES, 16, HALF), bf16),
            pltpu.VMEM((2, DEVICES // 2, 16, LATE * LANES), bf16),
            pltpu.VMEM((LATE, 128, LANES), f32),
            pltpu.VMEM((GROUPS, 4 * DEVICES, LANES), f32),
            pltpu.VMEM((2 * SPECTRA, SIGNALS), bf16),
            pltpu.VMEM((2 * SPECTRA, SIGNALS), bf16),
            pltpu.SemaphoreType.DMA(()),
            pltpu.SemaphoreType.DMA((2,)),
            pltpu.SemaphoreType.DMA((6,)),
            pltpu.SemaphoreType.DMA((6,)),
        ],
        compiler_params=pltpu.CompilerParams(
            collective_id=0, has_side_effects=True, vmem_limit_bytes=48 << 20
        ),
    )(voltages, filter_taps, jnp.asarray(fourier_rows()))
    kept = [pltpu.with_memory_space_constraint(array, pltpu.VMEM) for array in kept]
    return pl.pallas_call(
        finish,
        name="finish",
        out_shape=jax.ShapeDtypeStruct((2, 2, inputs, inputs), bf16),
        in_specs=[vmem] * 4,
        out_specs=anywhere,
        scratch_shapes=[
            pltpu.VMEM((2, SIGNALS, SIGNALS), bf16),
            pltpu.SemaphoreType.DMA(()),
            pltpu.SemaphoreType.DMA((SIGNALS // BLOCK,)),
        ],
        compiler_params=pltpu.CompilerParams(vmem_limit_bytes=48 << 20),
    )(*kept)


def solution(mesh):
    placed = (P(("row", "col"), None), P())
    return jax.shard_map(
        shards,
        mesh=mesh,
        in_specs=placed,
        out_specs=P(("row", "col"), None, None, None),
        check_vma=False,
    )
```

```python
import itertools

import jax
import jax.numpy as jnp
import numpy as np
from jax import lax
from jax.experimental import pallas as pl
from jax.experimental.pallas import tpu as pltpu
from jax.sharding import PartitionSpec as P

MESH = pl.DeviceIdType.MESH
DEVICES = 128
POINTS = 512
TAPS = 4
SPECTRA = 512
OWN = 4
LATE = TAPS - 1
SIGNALS = 1024
HALF = SIGNALS // 2
LANES = 128
GROUPS = SIGNALS // LANES
BLOCK = 256
STARTS = (0, 1024, 1792, 2304, 2560)


def orbit(offset):
    found = set()
    for turn in range(3):
        turned = offset[turn:] + offset[:turn]
        found.add(turned)
        found.add(tuple((-step) % 4 for step in turned))
    return tuple(sorted(found))


def send_order():
    hops = lambda group: sum(min(step, 4 - step) for step in group[0])
    groups = {orbit(offset) for offset in itertools.product(range(4), repeat=3)}
    ordered = []
    for group in sorted(sorted(groups), key=hops, reverse=True):
        for core in (0, 1):
            ordered += [offset + (core,) for offset in group]
    return [offset for offset in ordered if any(offset)]


ORDER = send_order()
CHIPS = list(dict.fromkeys(offset[:3] for offset in ORDER))
EDGES = (0, 22, 51, 64)
LOTS = [CHIPS[first:last] for first, last in zip(EDGES, EDGES[1:])]
SENDS = [[offset for offset in ORDER if offset[:3] in lot] for lot in LOTS]
LOT_SEM = (1, 4, 5)
LAST = 16 * len(LOTS[-1])


def coordinates():
    row, col = lax.axis_index("row"), lax.axis_index("col")
    return ((col // 2) % 2) * 2 + row // 4, row % 4, col // 4, col % 2


def partner(offset):
    place = coordinates()
    x, y, z = ((own + step) % 4 for own, step in zip(place[:3], offset[:3]))
    core = (place[3] + offset[3]) % 2
    return (x % 2) * 4 + y, z * 4 + (x // 2) * 2 + core


def fourier_rows():
    turns = np.arange(POINTS // 2)[:, None] * np.arange(POINTS)[None, :] % POINTS
    phase = turns.astype(np.float32) * np.float32(2.0 * np.pi / POINTS)
    scale = np.float32(1.0) / np.sqrt(np.float32(POINTS))
    table = np.stack([np.cos(phase), -np.sin(phase)], axis=1) * scale
    table = table.reshape(DEVICES, 2, 2, POINTS).transpose(1, 0, 2, 3)
    return table.reshape(2, POINTS // 2, POINTS).astype(jnp.bfloat16)


def correlate(x_ref, y_ref, depth, result, base=None, out_ref=None, sem=None):
    copies = []
    for step in range(SIGNALS // BLOCK):
        first, after = step * BLOCK, (step + 1) * BLOCK
        for part in range(2):
            product = block_row(x_ref, y_ref, depth, step, part)
            if base is not None:
                product = product + base[part, :, STARTS[step] : STARTS[step + 1]]
            product = (product * (1.0 / SPECTRA)).astype(jnp.bfloat16)
            result[part, first:after, first:] = product
            if after < SIGNALS:
                mirror = product[:, BLOCK:].T
                result[part, after:, first:after] = mirror if part == 0 else -mirror
        if out_ref is None:
            continue
        rows = pl.ds(first, BLOCK)
        copy = pltpu.make_async_copy(result.at[:, rows], out_ref.at[:, rows], sem.at[step])
        copy.start()
        copies.append(copy)
    return copies


def block_row(x_ref, y_ref, depth, step, part):
    left = y_ref if part else x_ref
    return lax.dot_general(
        left[0:depth, step * BLOCK : (step + 1) * BLOCK],
        x_ref[0:depth, step * BLOCK :],
        (((0,), (0,)), ((), ())),
        preferred_element_type=jnp.float32,
    )


def spread(
    volt_ref, taps_ref, table_ref, result, sums, x_last, y_last,
    frames, weights, filtered, main, tails, outbox, outbox_late, inbox, inbox_late, lifted, added, x_ref, y_ref,
    near_sem, pair_sem, send_sem, recv_sem,
):
    row, col = lax.axis_index("row"), lax.axis_index("col")
    me = row * 16 + col
    core = col % 2
    near = []
    for half in range(2):
        lanes = pl.ds(half * HALF, HALF)
        own = frames.at[pl.ds(LATE * POINTS, OWN * POINTS), lanes]
        near.append(pltpu.make_async_copy(volt_ref.at[:, lanes], own, near_sem.at[half]))
        near[half].start()
    barrier = pltpu.get_barrier_semaphore()
    for offset in ORDER:
        pl.semaphore_signal(barrier, inc=1, device_id=partner(offset), device_id_type=MESH)

    padded = jnp.concatenate([taps_ref[...], jnp.zeros((LANES - TAPS, POINTS), jnp.float32)], axis=0)
    for first in range(0, POINTS, LANES):
        columns = padded[:, first : first + LANES].T
        for tap in range(TAPS):
            weights[tap, first : first + LANES, :] = jnp.broadcast_to(columns[:, tap : tap + 1], (LANES, LANES))
    added[...] = jnp.zeros(added.shape, jnp.float32)
    halo = pltpu.make_async_remote_copy(
        src_ref=volt_ref.at[pl.ds((OWN - LATE) * POINTS, LATE * POINTS)],
        dst_ref=frames.at[pl.ds(0, LATE * POINTS)],
        send_sem=pair_sem.at[0],
        recv_sem=pair_sem.at[1],
        device_id=partner((0, 0, 0, 1)),
        device_id_type=MESH,
    )

    def filter_frames(outputs, slots, half):
        def rows16(step, carry):
            rows = pl.ds(pl.multiple_of(step * 16, 16), 16)
            taps = [jnp.concatenate([weights[tap, rows, :]] * 2, axis=1) for tap in range(TAPS)]
            for left in range(half * HALF, (half + 1) * HALF, 256):
                lanes = slice(left, left + 256)
                values = {}
                for slot in slots:
                    at = pl.ds(pl.multiple_of(slot * POINTS + step * 16, 16), 16)
                    values[slot] = frames[at, lanes].astype(jnp.float32)
                for frame in outputs:
                    total = None
                    for tap in range(TAPS):
                        if frame + tap in values:
                            term = taps[tap] * values[frame + tap]
                            total = term if total is None else total + term
                    filtered[frame, rows, lanes] = total.astype(jnp.bfloat16)
            return carry

        lax.fori_loop(0, POINTS // 16, rows16, 0)

    def transform(channel, half, frame):
        values = filtered[frame, :, half * HALF : (half + 1) * HALF]
        return jnp.dot(table_ref[channel], values, preferred_element_type=jnp.float32)

    def transform_main(channel, half):
        def one(frame, carry):
            spectrum = transform(channel, half, frame)
            for group in range(GROUPS // 2):
                rows = pl.ds(frame, 2 * DEVICES, stride=OWN)
                main[half * (GROUPS // 2) + group, rows, :] = spectrum[:, group * LANES : (group + 1) * LANES]
            return carry

        lax.fori_loop(0, OWN, one, 0)

    def transform_late(channel, half):
        def one(late, carry):
            spectrum = transform(channel, half, late + OWN)
            for group in range(GROUPS // 2):
                rows = pl.ds(half * (GROUPS // 2) + group, 2 * DEVICES, stride=GROUPS)
                tails[late, rows, :] = spectrum[:, group * LANES : (group + 1) * LANES]
            return carry

        lax.fori_loop(0, LATE, one, 0)

    def pack_main(channel, target):
        rows = pl.ds(pl.multiple_of(target * 8, 8), 8)
        for group in range(GROUPS // 2):
            both = jnp.concatenate([main[group, rows, :], main[group + GROUPS // 2, rows, :]], axis=0)
            outbox[channel, target, :, group * LANES : (group + 1) * LANES] = both.astype(jnp.bfloat16)

    def pack_late(channel, target):
        rows = pl.ds(pl.multiple_of(target * 16, 16), 16)
        for late in range(LATE):
            outbox_late[channel, target, :, late * LANES : (late + 1) * LANES] = tails[late, rows, :].astype(
                jnp.bfloat16
            )

    def pack_all(pack, channel):
        def one(target, carry):
            pack(channel, target)
            return carry

        lax.fori_loop(0, DEVICES, one, 0, unroll=8)

    def send(channel, box, into, place, sem, order=ORDER):
        for offset in order:
            to = partner(offset)
            target = to[0] * 16 + to[1]
            pltpu.make_async_remote_copy(
                src_ref=box.at[channel, target],
                dst_ref=into.at[channel, place],
                send_sem=send_sem.at[sem],
                recv_sem=recv_sem.at[sem],
                device_id=to,
                device_id_type=MESH,
            ).start()

    def arrived(channel, count, sem):
        most = inbox.at[channel, pl.ds(0, count)]
        pltpu.make_async_copy(most, most, recv_sem.at[sem]).wait()

    def arrived_late(channel):
        @pl.when(core == 0)
        def _():
            late = inbox_late.at[channel]
            pltpu.make_async_copy(late, late, recv_sem.at[2 + channel]).wait()

        @pl.when(core == 1)
        def _():
            late = inbox_late.at[channel, pl.ds(0, DEVICES // 2 - 1)]
            pltpu.make_async_copy(late, late, recv_sem.at[2 + channel]).wait()

    def lift(channel):
        def eight(step, carry):
            for index in range(8):
                chip = step * 8 + index
                before = jnp.maximum(chip - 1, 0)
                for late in range(LATE):
                    tail = inbox_late[channel, before, :, late * LANES : (late + 1) * LANES].astype(jnp.float32)
                    lifted[late, index * 16 : (index + 1) * 16, :] = jnp.where(chip > 0, tail, 0.0)
            for late in range(LATE):
                for group in range(GROUPS):
                    rows = pl.ds(step * 64 + late, 16, stride=OWN)
                    added[group, rows, :] = lifted[late, pl.ds(group, 16, stride=GROUPS), :]
            return carry

        lax.fori_loop(0, DEVICES // 16, eight, 0)

    def merge(channel, chip, rows, x_to, y_to):
        row_of = lax.broadcasted_iota(jnp.int32, (16, LANES), 0)
        sign = jnp.where(row_of % 8 < OWN, 1.0, -1.0).astype(jnp.float32)
        extra_rows = pl.ds(pl.multiple_of(chip * 8, 8), 8)
        for group in range(GROUPS // 2):
            lanes = slice(group * LANES, (group + 1) * LANES)
            lower = inbox[channel, 2 * chip, :, lanes].astype(jnp.float32)
            upper = inbox[channel, 2 * chip + 1, :, lanes].astype(jnp.float32)
            for half in range(2):
                whole = half * (GROUPS // 2) + group
                part = slice(half * 8, half * 8 + 8)
                early = lower[part] + added[whole, extra_rows, :]
                value = jnp.concatenate([early, upper[part]], axis=0)
                turned = jnp.concatenate([pltpu.roll(early, OWN, 0), pltpu.roll(upper[part], OWN, 0)], axis=0)
                out = slice(whole * LANES, (whole + 1) * LANES)
                x_to[rows, out] = value.astype(jnp.bfloat16)
                y_to[rows, out] = (turned * sign).astype(jnp.bfloat16)

    def merge_whole(channel):
        def eight(step, carry):
            for index in range(8):
                chip = step * 8 + index
                merge(channel, chip, pl.ds(pl.multiple_of(chip * 16, 16), 16), x_ref, y_ref)
            return carry

        lax.fori_loop(0, DEVICES // 16, eight, 0)

    def merge_lot(channel, lot, x_to, y_to):
        for index, offset in enumerate(LOTS[lot]):
            place = partner(offset + (0,))
            merge(channel, place[0] * 8 + place[1] // 2, slice(index * 16, index * 16 + 16), x_to, y_to)

    @pl.when(core == 0)
    def _():
        frames[0 : LATE * POINTS, :] = jnp.zeros((LATE * POINTS, SIGNALS), jnp.bfloat16)
        for half in range(2):
            near[half].wait()
            filter_frames(range(OWN), range(OWN + LATE), half)
            transform_main(0, half)
        pack_all(pack_main, 0)
        pl.semaphore_wait(barrier, len(ORDER))
        halo.start()
        send(0, outbox, inbox, me, 0)

    @pl.when(core == 1)
    def _():
        for half in range(2):
            near[half].wait()
            filter_frames(range(OWN, OWN + LATE), range(OWN, OWN + LATE), half)
            transform_late(0, half)
        pack_all(pack_late, 0)
        pl.semaphore_wait(barrier, len(ORDER))
        send(0, outbox_late, inbox_late, me // 2, 2)
        inbox_late[0, me // 2] = outbox_late[0, me]
        halo.wait_recv()
        for half in range(2):
            filter_frames(range(OWN), range(OWN + LATE), half)
            transform_main(0, half)
        pack_all(pack_main, 0)
        send(0, outbox, inbox, me, 0)
        for half in range(2):
            transform_late(1, half)
        pack_all(pack_late, 1)
        send(1, outbox_late, inbox_late, me // 2, 3)
        inbox_late[1, me // 2] = outbox_late[1, me]

    inbox[0, me] = outbox[0, me]
    for half in range(2):
        transform_main(1, half)
    pack_all(pack_main, 1)
    for sends, sem in zip(SENDS, LOT_SEM):
        send(1, outbox, inbox, me, sem, sends)
    inbox[1, me] = outbox[1, me]

    arrived(0, DEVICES - 1, 0)
    arrived_late(0)
    lift(0)
    merge_whole(0)
    correlate(x_ref, y_ref, 2 * SPECTRA, result)
    arrived_late(1)
    lift(1)
    for lot in range(len(LOTS) - 1):
        arrived(1, len(SENDS[lot]), LOT_SEM[lot])
        merge_lot(1, lot, x_ref, y_ref)
        for step in range(SIGNALS // BLOCK):
            columns = slice(STARTS[step], STARTS[step + 1])
            for part in range(2):
                product = block_row(x_ref, y_ref, 16 * len(LOTS[lot]), step, part)
                sums[part, :, columns] = product if lot == 0 else sums[part, :, columns] + product
    arrived(1, len(SENDS[-1]), LOT_SEM[-1])
    merge_lot(1, len(LOTS) - 1, x_last, y_last)
    for channel, count, sem in [(0, DEVICES - 1, 0)] + [(1, len(sends), sem) for sends, sem in zip(SENDS, LOT_SEM)]:
        most = outbox.at[channel, pl.ds(0, count)]
        pltpu.make_async_copy(most, most, send_sem.at[sem]).wait()

    @pl.when(core == 0)
    def _():
        halo.wait_send()

    @pl.when(core == 1)
    def _():
        for channel in range(2):
            most = outbox_late.at[channel, pl.ds(0, DEVICES - 1)]
            pltpu.make_async_copy(most, most, send_sem.at[2 + channel]).wait()


def finish(vis_ref, sums, x_ref, y_ref, out_ref, result, done_sem, out_sem):
    done = pltpu.make_async_copy(vis_ref, out_ref.at[0], done_sem)
    done.start()
    for copy in correlate(x_ref, y_ref, LAST, result, sums, out_ref.at[1], out_sem):
        copy.wait()
    done.wait()


def shards(voltages, filter_taps):
    inputs = voltages.shape[1]
    vmem = pl.BlockSpec(memory_space=pltpu.VMEM)
    anywhere = pl.BlockSpec(memory_space=pl.ANY)
    bf16, f32 = jnp.bfloat16, jnp.float32
    last = pltpu.VMEM((LAST, inputs), bf16)
    kept = [pltpu.VMEM((2, inputs, inputs), bf16), pltpu.VMEM((2, BLOCK, STARTS[-1]), f32), last, last]
    kept = pl.pallas_call(
        spread,
        name="spread",
        out_shape=kept,
        in_specs=[anywhere, vmem, vmem],
        out_specs=[vmem] * 4,
        scratch_shapes=[
            pltpu.VMEM(((OWN + LATE) * POINTS, SIGNALS), bf16),
            pltpu.VMEM((TAPS, POINTS, LANES), f32),
            pltpu.VMEM((OWN + LATE, POINTS, SIGNALS), bf16),
            pltpu.VMEM((GROUPS, DEVICES * 2 * OWN, LANES), f32),
            pltpu.VMEM((LATE, DEVICES * 2 * GROUPS, LANES), f32),
            pltpu.VMEM((2, DEVICES, 16, HALF), bf16),
            pltpu.VMEM((2, DEVICES, 16, LATE * LANES), bf16),
            pltpu.VMEM((2, DEVICES, 16, HALF), bf16),
            pltpu.VMEM((2, DEVICES // 2, 16, LATE * LANES), bf16),
            pltpu.VMEM((LATE, 128, LANES), f32),
            pltpu.VMEM((GROUPS, 4 * DEVICES, LANES), f32),
            pltpu.VMEM((2 * SPECTRA, SIGNALS), bf16),
            pltpu.VMEM((2 * SPECTRA, SIGNALS), bf16),
            pltpu.SemaphoreType.DMA((2,)),
            pltpu.SemaphoreType.DMA((2,)),
            pltpu.SemaphoreType.DMA((6,)),
            pltpu.SemaphoreType.DMA((6,)),
        ],
        compiler_params=pltpu.CompilerParams(
            collective_id=0, has_side_effects=True, vmem_limit_bytes=48 << 20
        ),
    )(voltages, filter_taps, jnp.asarray(fourier_rows()))
    kept = [pltpu.with_memory_space_constraint(array, pltpu.VMEM) for array in kept]
    return pl.pallas_call(
        finish,
        name="finish",
        out_shape=jax.ShapeDtypeStruct((2, 2, inputs, inputs), bf16),
        in_specs=[vmem] * 4,
        out_specs=anywhere,
        scratch_shapes=[
            pltpu.VMEM((2, SIGNALS, SIGNALS), bf16),
            pltpu.SemaphoreType.DMA(()),
            pltpu.SemaphoreType.DMA((SIGNALS // BLOCK,)),
        ],
        compiler_params=pltpu.CompilerParams(vmem_limit_bytes=48 << 20),
    )(*kept)


def solution(mesh):
    placed = (P(("row", "col"), None), P())
    return jax.shard_map(
        shards,
        mesh=mesh,
        in_specs=placed,
        out_specs=P(("row", "col"), None, None, None),
        check_vma=False,
    )
```

```python
import itertools

import jax
import jax.numpy as jnp
import numpy as np
from jax import lax
from jax.experimental import pallas as pl
from jax.experimental.pallas import tpu as pltpu
from jax.sharding import PartitionSpec as P

MESH = pl.DeviceIdType.MESH
DEVICES = 128
POINTS = 512
TAPS = 4
SPECTRA = 512
OWN = 4
LATE = TAPS - 1
SIGNALS = 1024
HALF = SIGNALS // 2
LANES = 128
GROUPS = SIGNALS // LANES
BLOCK = 256


def orbit(offset):
    found = set()
    for turn in range(3):
        turned = offset[turn:] + offset[:turn]
        found.add(turned)
        found.add(tuple((-step) % 4 for step in turned))
    return tuple(sorted(found))


def send_order():
    hops = lambda group: sum(min(step, 4 - step) for step in group[0])
    groups = {orbit(offset) for offset in itertools.product(range(4), repeat=3)}
    ordered = []
    for group in sorted(sorted(groups), key=hops, reverse=True):
        for core in (0, 1):
            ordered += [offset + (core,) for offset in group]
    return [offset for offset in ordered if any(offset)]


ORDER = send_order()
NEAR = 84


def coordinates():
    row, col = lax.axis_index("row"), lax.axis_index("col")
    return ((col // 2) % 2) * 2 + row // 4, row % 4, col // 4, col % 2


def partner(offset):
    place = coordinates()
    x, y, z = ((own + step) % 4 for own, step in zip(place[:3], offset[:3]))
    core = (place[3] + offset[3]) % 2
    return (x % 2) * 4 + y, z * 4 + (x // 2) * 2 + core


def entry(place):
    row, col = place
    return (col // 2 % 2) * 2 + row // 4 + row % 4 + 2 * (col // 4)


def fourier_rows():
    turns = np.arange(POINTS // 2)[:, None] * np.arange(POINTS)[None, :] % POINTS
    phase = turns.astype(np.float32) * np.float32(2.0 * np.pi / POINTS)
    scale = np.float32(1.0) / np.sqrt(np.float32(POINTS))
    table = np.stack([np.cos(phase), -np.sin(phase)], axis=1) * scale
    table = table.reshape(DEVICES, 2, 2, POINTS).transpose(1, 0, 2, 3)
    return table.reshape(2, POINTS // 2, POINTS).astype(jnp.bfloat16)


def correlate(x_ref, y_ref, result, out_ref=None, sem=None):
    dims = (((0,), (0,)), ((), ()))
    copies = []
    for step in range(SIGNALS // BLOCK):
        first, after = step * BLOCK, (step + 1) * BLOCK
        for part, left in enumerate((x_ref, y_ref)):
            product = lax.dot_general(
                left[:, first:after], x_ref[:, first:], dims, preferred_element_type=jnp.float32
            )
            product = (product * (1.0 / SPECTRA)).astype(jnp.bfloat16)
            result[part, first:after, first:] = product
            if after < SIGNALS:
                mirror = product[:, BLOCK:].T
                result[part, after:, first:after] = mirror if part == 0 else -mirror
        if out_ref is None:
            continue
        rows = pl.ds(first, BLOCK)
        copy = pltpu.make_async_copy(result.at[:, rows], out_ref.at[:, rows], sem.at[step])
        copy.start()
        copies.append(copy)
    return copies


def spread(
    volt_ref, taps_ref, table_ref, result, x_ref, y_ref,
    frames, weights, filtered, main, tails, outbox, outbox_late, inbox, inbox_late, lifted, added,
    near_sem, pair_sem, send_sem, recv_sem,
):
    row, col = lax.axis_index("row"), lax.axis_index("col")
    me = row * 16 + col
    core = col % 2
    near = pltpu.make_async_copy(volt_ref, frames.at[pl.ds(LATE * POINTS, OWN * POINTS)], near_sem)
    near.start()
    barrier = pltpu.get_barrier_semaphore()
    for offset in ORDER:
        pl.semaphore_signal(barrier, inc=1, device_id=partner(offset), device_id_type=MESH)

    padded = jnp.concatenate([taps_ref[...], jnp.zeros((LANES - TAPS, POINTS), jnp.float32)], axis=0)
    for first in range(0, POINTS, LANES):
        columns = padded[:, first : first + LANES].T
        for tap in range(TAPS):
            weights[tap, first : first + LANES, :] = jnp.broadcast_to(columns[:, tap : tap + 1], (LANES, LANES))
    added[...] = jnp.zeros(added.shape, jnp.float32)
    halo = pltpu.make_async_remote_copy(
        src_ref=volt_ref.at[pl.ds((OWN - LATE) * POINTS, LATE * POINTS)],
        dst_ref=frames.at[pl.ds(0, LATE * POINTS)],
        send_sem=pair_sem.at[0],
        recv_sem=pair_sem.at[1],
        device_id=partner((0, 0, 0, 1)),
        device_id_type=MESH,
    )

    def filter_frames(outputs, slots):
        def rows16(step, carry):
            rows = pl.ds(pl.multiple_of(step * 16, 16), 16)
            taps = [jnp.concatenate([weights[tap, rows, :]] * 2, axis=1) for tap in range(TAPS)]
            for left in range(0, SIGNALS, 256):
                lanes = slice(left, left + 256)
                values = {}
                for slot in slots:
                    at = pl.ds(pl.multiple_of(slot * POINTS + step * 16, 16), 16)
                    values[slot] = frames[at, lanes].astype(jnp.float32)
                for frame in outputs:
                    total = None
                    for tap in range(TAPS):
                        if frame + tap in values:
                            term = taps[tap] * values[frame + tap]
                            total = term if total is None else total + term
                    filtered[frame, rows, lanes] = total.astype(jnp.bfloat16)
            return carry

        lax.fori_loop(0, POINTS // 16, rows16, 0)

    def transform(channel, index, frame):
        half = index % 2
        lanes = pl.ds(pl.multiple_of(half * HALF, HALF), HALF)
        return half, jnp.dot(table_ref[channel], filtered[frame, :, lanes], preferred_element_type=jnp.float32)

    def transform_main(channel):
        def one(index, carry):
            frame = index // 2
            half, spectrum = transform(channel, index, frame)
            for group in range(GROUPS // 2):
                rows = pl.ds(frame, 2 * DEVICES, stride=OWN)
                main[half * (GROUPS // 2) + group, rows, :] = spectrum[:, group * LANES : (group + 1) * LANES]
            return carry

        lax.fori_loop(0, 2 * OWN, one, 0)

    def transform_late(channel):
        def one(index, carry):
            late = index // 2
            half, spectrum = transform(channel, index, late + OWN)
            for group in range(GROUPS // 2):
                rows = pl.ds(half * (GROUPS // 2) + group, 2 * DEVICES, stride=GROUPS)
                tails[late, rows, :] = spectrum[:, group * LANES : (group + 1) * LANES]
            return carry

        lax.fori_loop(0, 2 * LATE, one, 0)

    def pack_main(channel):
        def one(target, carry):
            rows = pl.ds(pl.multiple_of(target * 8, 8), 8)
            for group in range(GROUPS // 2):
                both = jnp.concatenate([main[group, rows, :], main[group + GROUPS // 2, rows, :]], axis=0)
                outbox[channel, target, :, group * LANES : (group + 1) * LANES] = both.astype(jnp.bfloat16)
            return carry

        lax.fori_loop(0, DEVICES, one, 0, unroll=4)

    def pack_late(channel):
        def one(target, carry):
            rows = pl.ds(pl.multiple_of(target * 16, 16), 16)
            for late in range(LATE):
                outbox_late[channel, target, :, late * LANES : (late + 1) * LANES] = tails[late, rows, :].astype(
                    jnp.bfloat16
                )
            return carry

        lax.fori_loop(0, DEVICES, one, 0, unroll=4)

    def send_to(channel, box, into, place, sem, to):
        pltpu.make_async_remote_copy(
            src_ref=box.at[channel, to[0] * 16 + to[1]],
            dst_ref=into.at[channel, place],
            send_sem=send_sem.at[sem],
            recv_sem=recv_sem.at[sem],
            device_id=to,
            device_id_type=MESH,
        ).start()

    def send(channel, box, into, place, sem, order=ORDER):
        for offset in order:
            send_to(channel, box, into, place, sem, partner(offset))

    def arrived(channel):
        most = inbox.at[channel, pl.ds(0, DEVICES - 1)]
        pltpu.make_async_copy(most, most, recv_sem.at[channel]).wait()

        @pl.when(core == 0)
        def _():
            late = inbox_late.at[channel]
            pltpu.make_async_copy(late, late, recv_sem.at[2 + channel]).wait()

        @pl.when(core == 1)
        def _():
            late = inbox_late.at[channel, pl.ds(0, DEVICES // 2 - 1)]
            pltpu.make_async_copy(late, late, recv_sem.at[2 + channel]).wait()

    def merge(channel):
        row_of = lax.broadcasted_iota(jnp.int32, (16, LANES), 0)
        sign = jnp.where(row_of % 8 < OWN, 1.0, -1.0).astype(jnp.float32)

        def eight(step, carry):
            first = step * 8
            for index in range(8):
                chip = first + index
                before = jnp.maximum(chip - 1, 0)
                for late in range(LATE):
                    tail = inbox_late[channel, before, :, late * LANES : (late + 1) * LANES].astype(jnp.float32)
                    lifted[late, index * 16 : (index + 1) * 16, :] = jnp.where(chip > 0, tail, 0.0)
            for late in range(LATE):
                for group in range(GROUPS):
                    added[group, pl.ds(late, 16, stride=OWN), :] = lifted[late, pl.ds(group, 16, stride=GROUPS), :]
            for index in range(8):
                chip = first + index
                rows = pl.ds(pl.multiple_of(chip * 16, 16), 16)
                for group in range(GROUPS // 2):
                    lanes = slice(group * LANES, (group + 1) * LANES)
                    lower = inbox[channel, 2 * chip, :, lanes].astype(jnp.float32)
                    upper = inbox[channel, 2 * chip + 1, :, lanes].astype(jnp.float32)
                    for half in range(2):
                        whole = half * (GROUPS // 2) + group
                        extra = added[whole, index * 8 : index * 8 + 8, :]
                        part = slice(half * 8, half * 8 + 8)
                        early = lower[part] + extra
                        value = jnp.concatenate([early, upper[part]], axis=0)
                        turned = jnp.concatenate(
                            [pltpu.roll(early, OWN, 0), pltpu.roll(upper[part], OWN, 0)], axis=0
                        )
                        out = slice(whole * LANES, (whole + 1) * LANES)
                        x_ref[rows, out] = value.astype(jnp.bfloat16)
                        y_ref[rows, out] = (turned * sign).astype(jnp.bfloat16)
            return carry

        lax.fori_loop(0, DEVICES // 16, eight, 0)

    near.wait()

    @pl.when(core == 0)
    def _():
        frames[0 : LATE * POINTS, :] = jnp.zeros((LATE * POINTS, SIGNALS), jnp.bfloat16)
        filter_frames(range(OWN), range(OWN + LATE))
        transform_main(0)
        pack_main(0)
        pl.semaphore_wait(barrier, len(ORDER))
        halo.start()
        send(0, outbox, inbox, me, 0)

    @pl.when(core == 1)
    def _():
        filter_frames(range(OWN, OWN + LATE), range(OWN, OWN + LATE))
        transform_late(0)
        pack_late(0)
        pl.semaphore_wait(barrier, len(ORDER))
        send(0, outbox_late, inbox_late, me // 2, 2)
        inbox_late[0, me // 2] = outbox_late[0, me]
        halo.wait_recv()
        filter_frames(range(OWN), range(OWN + LATE))
        transform_main(0)
        pack_main(0)
        send(0, outbox, inbox, me, 0)
        transform_late(1)
        pack_late(1)
        send(1, outbox_late, inbox_late, me // 2, 3)
        inbox_late[1, me // 2] = outbox_late[1, me]

    inbox[0, me] = outbox[0, me]
    transform_main(1)
    pack_main(1)
    send(1, outbox, inbox, me, 1, ORDER[:NEAR])
    for later in range(2):
        for offset in ORDER[NEAR:]:
            mirrored = tuple((-step) % 4 for step in offset[:3]) + offset[3:]
            if mirrored > offset or (mirrored == offset and not later):
                one, two = partner(offset), partner(mirrored)
                swap = (entry(one) > entry(two)).astype(jnp.int32)
                swap = 1 - swap if later else swap
                to = tuple(first + swap * (second - first) for first, second in zip(one, two))
                send_to(1, outbox, inbox, me, 1, to)
    inbox[1, me] = outbox[1, me]

    arrived(0)
    merge(0)
    correlate(x_ref, y_ref, result)
    arrived(1)
    merge(1)
    for channel in range(2):
        most = outbox.at[channel, pl.ds(0, DEVICES - 1)]
        pltpu.make_async_copy(most, most, send_sem.at[channel]).wait()

    @pl.when(core == 0)
    def _():
        halo.wait_send()

    @pl.when(core == 1)
    def _():
        for channel in range(2):
            most = outbox_late.at[channel, pl.ds(0, DEVICES - 1)]
            pltpu.make_async_copy(most, most, send_sem.at[2 + channel]).wait()


def finish(vis_ref, x_ref, y_ref, out_ref, result, done_sem, out_sem):
    done = pltpu.make_async_copy(vis_ref, out_ref.at[0], done_sem)
    done.start()
    for copy in correlate(x_ref, y_ref, result, out_ref.at[1], out_sem):
        copy.wait()
    done.wait()


def shards(voltages, filter_taps):
    inputs = voltages.shape[1]
    vmem = pl.BlockSpec(memory_space=pltpu.VMEM)
    anywhere = pl.BlockSpec(memory_space=pl.ANY)
    bf16, f32 = jnp.bfloat16, jnp.float32
    square = pltpu.VMEM((2 * SPECTRA, inputs), bf16)
    kept = [pltpu.VMEM((2, inputs, inputs), bf16), square, square]
    kept = pl.pallas_call(
        spread,
        name="spread",
        out_shape=kept,
        in_specs=[anywhere, vmem, vmem],
        out_specs=[vmem] * 3,
        scratch_shapes=[
            pltpu.VMEM(((OWN + LATE) * POINTS, SIGNALS), bf16),
            pltpu.VMEM((TAPS, POINTS, LANES), f32),
            pltpu.VMEM((OWN + LATE, POINTS, SIGNALS), bf16),
            pltpu.VMEM((GROUPS, DEVICES * 2 * OWN, LANES), f32),
            pltpu.VMEM((LATE, DEVICES * 2 * GROUPS, LANES), f32),
            pltpu.VMEM((2, DEVICES, 16, HALF), bf16),
            pltpu.VMEM((2, DEVICES, 16, LATE * LANES), bf16),
            pltpu.VMEM((2, DEVICES, 16, HALF), bf16),
            pltpu.VMEM((2, DEVICES // 2, 16, LATE * LANES), bf16),
            pltpu.VMEM((LATE, 128, LANES), f32),
            pltpu.VMEM((GROUPS, 64, LANES), f32),
            pltpu.SemaphoreType.DMA(()),
            pltpu.SemaphoreType.DMA((2,)),
            pltpu.SemaphoreType.DMA((4,)),
            pltpu.SemaphoreType.DMA((4,)),
        ],
        compiler_params=pltpu.CompilerParams(
            collective_id=0, has_side_effects=True, vmem_limit_bytes=50 << 20
        ),
    )(voltages, filter_taps, jnp.asarray(fourier_rows()))
    kept = [pltpu.with_memory_space_constraint(array, pltpu.VMEM) for array in kept]
    return pl.pallas_call(
        finish,
        name="finish",
        out_shape=jax.ShapeDtypeStruct((2, 2, inputs, inputs), bf16),
        in_specs=[vmem] * 3,
        out_specs=anywhere,
        scratch_shapes=[
            pltpu.VMEM((2, SIGNALS, SIGNALS), bf16),
            pltpu.SemaphoreType.DMA(()),
            pltpu.SemaphoreType.DMA((SIGNALS // BLOCK,)),
        ],
        compiler_params=pltpu.CompilerParams(vmem_limit_bytes=48 << 20),
    )(*kept)


def solution(mesh):
    placed = (P(("row", "col"), None), P())
    return jax.shard_map(
        shards,
        mesh=mesh,
        in_specs=placed,
        out_specs=P(("row", "col"), None, None, None),
        check_vma=False,
    )
```
